512 devices in a mesh: gx: 32 (over y, x, z_hi), gy: 16 (over z_lo, core).
Axes of the slice: x: 4, y: 4, z: 16 (z_hi: 2, z_lo: 8; z = z_hi * 8 + z_lo), core: 2. Of those that a mesh axis runs over, the one named last changes fastest.
Arguments:
- picture_embedding_matrix: bfloat16 [262144, 1152], P(('gx', 'gy')), may hold values from -6 to 6
- caption_embedding_matrix: bfloat16 [262144, 1152], P(('gx', 'gy')), may hold values from -6 to 6
- score_scale: float32 [1], replicated, may hold values from 10 to 40
- logit_offset: float32 [1], replicated, may hold values from -4 to -1
Outputs:
- row_loss: float32 [262144], P(('gx', 'gy'))
- image_grad: bfloat16 [262144, 1152], P(('gx', 'gy'))
- text_grad: bfloat16 [262144, 1152], P(('gx', 'gy'))
The draws below stay inside these ranges and needn't reach their ends.
All inputs are finite; a program needn't handle non-finite values.
Results may differ from the reference program's by a relative error of at most 0.0074.
Values may be sent and summed in bfloat16 or wider, within the bound.
A program may use at most 64 MiB of HBM per device.

```python
import math
import jax
import jax.numpy as jnp
from jax import lax

D = 1152
ROWS = 512
PAIRS = 262144
N_GX = 32
N_GY = 16


def steps_of(own_key, dims, cuts, low, largest):
    level, own = 1.0, jax.random.fold_in(own_key, 6)
    for dim, blocks in cuts:
        draws = jnp.exp(jax.random.uniform(jax.random.fold_in(own, dim), (blocks,), jnp.float32, low / len(cuts), largest / len(cuts)))
        level = level * jnp.repeat(draws, dims[dim] // blocks).reshape([-1 if axis == dim else 1 for axis in range(len(dims))])
    return level


def gaussian(rng, extent, scale, reach, split=(), held_as=jnp.bfloat16):
    values = jax.random.normal(rng, extent, jnp.float32) * scale
    if len(split) > 0:
        values = steps_of(rng, extent, split, -0.22, 0.18) * values
    return jnp.clip(values, min=-reach, max=reach).astype(held_as)


def setup_inputs(seed: int = 0) -> dict:
    seeds = jax.random.split(jax.random.key(seed), 5)
    picture_embedding_matrix = gaussian(seeds[0], (PAIRS, D), 1.0, 6.0, ((0, 512),))
    caption_embedding_matrix = gaussian(seeds[1], (PAIRS, D), 1.0, 6.0, ((0, 512),))
    score_scale = jnp.clip(jnp.exp(jax.random.uniform(seeds[2], (1,), jnp.float32, math.log(10.0), math.log(40.0))), 10.0, 40.0)
    logit_offset = jnp.clip(jax.random.uniform(seeds[3], (1,), jnp.float32, -4.0, -1.0), -4.0, -1.0)
    return {"picture_embedding_matrix": picture_embedding_matrix, "caption_embedding_matrix": caption_embedding_matrix, "score_scale": score_scale, "logit_offset": logit_offset}


def normalize(raw):
    wide = raw.astype(jnp.float32)
    inverse = lax.rsqrt(lax.optimization_barrier(jnp.sum(wide * wide, axis=-1, keepdims=True)) + 1e-06)
    return ((wide * inverse).astype(jnp.bfloat16), inverse, wide * inverse)

def couple_tile_objective(picture_tile_entries, caption_tile_entries, matching_couple, score_scale, logit_offset):
    couple_scores = score_scale[0] * jnp.dot(picture_tile_entries, caption_tile_entries.T, preferred_element_type=jnp.float32) + logit_offset[0]
    count = couple_scores.shape[0]
    same = jnp.arange(count)[:, None] == jnp.arange(count)[None, :]
    match_polarity = jnp.where(jnp.logical_and(same, matching_couple), 1.0, -1.0).astype(jnp.float32)
    block_losses = jax.nn.softplus(-match_polarity * couple_scores)
    objective_weight = (-score_scale[0] * match_polarity * jax.nn.sigmoid(-match_polarity * couple_scores)).astype(jnp.bfloat16)
    img_part = jnp.dot(objective_weight, caption_tile_entries, preferred_element_type=jnp.float32)
    txt_part = jnp.dot(objective_weight.T, picture_tile_entries, preferred_element_type=jnp.float32)
    return (lax.optimization_barrier(jnp.sum(block_losses, axis=1)), img_part, txt_part)

def backnorm(inverse, unit, direction):
    return (inverse * (direction - unit * lax.optimization_barrier(jnp.sum(unit * direction, axis=-1, keepdims=True)))).astype(jnp.bfloat16)

def reference(picture_embedding_matrix, caption_embedding_matrix, score_scale, logit_offset):
    picture_unit_vectors, inv_img, img_unit = normalize(picture_embedding_matrix)
    txt_n, inv_txt, txt_unit = normalize(caption_embedding_matrix)
    width = picture_embedding_matrix.shape[1]
    img_b = picture_unit_vectors.reshape(N_GX, N_GY, ROWS, width)
    txt_b = txt_n.reshape(N_GX, N_GY, ROWS, width)
    loss_sum = jnp.zeros((N_GX, N_GY, ROWS), jnp.float32)
    img_dir = jnp.zeros((N_GX, N_GY, ROWS, width), jnp.float32)
    txt_dir = jnp.zeros((N_GX, N_GY, ROWS, width), jnp.float32)
    for shift_x, shift_y in ((0, 0), (1, 0), (0, 1), (1, 1)):
        covered_couples = jnp.roll(txt_b, (shift_x, shift_y), axis=(0, 1))
        matching_couple = shift_x == 0 and shift_y == 0

        def one(objective_shares):
            return couple_tile_objective(objective_shares[0], objective_shares[1], matching_couple, score_scale, logit_offset)
        block_losses, img_part, txt_part = lax.map(one, (img_b.reshape(-1, ROWS, width), covered_couples.reshape(-1, ROWS, width)))
        if not matching_couple:
            txt_part = lax.optimization_barrier(txt_part.astype(jnp.bfloat16)).astype(jnp.float32)
        loss_sum = loss_sum + block_losses.reshape(N_GX, N_GY, ROWS)
        img_dir = img_dir + img_part.reshape(N_GX, N_GY, ROWS, width)
        txt_dir = txt_dir + jnp.roll(txt_part.reshape(N_GX, N_GY, ROWS, width), (-shift_x, -shift_y), axis=(0, 1))
    row_loss = loss_sum.reshape(-1) / (4.0 * ROWS)
    image_grad = backnorm(inv_img, img_unit, img_dir.reshape(-1, width))
    text_grad = backnorm(inv_txt, txt_unit, txt_dir.reshape(-1, width))
    return (row_loss, image_grad, text_grad)
```

```python
import jax
import jax.numpy as jnp
from jax import lax
from jax.experimental import pallas as pl
from jax.experimental.pallas import tpu as pltpu
from jax.sharding import PartitionSpec as P

MESH = pl.DeviceIdType.MESH
F32 = jnp.float32
BF16 = jnp.bfloat16

TXT, IMG = 0, 1
HOPS = 8
CHUNKS = 4
FIN_ROWS = 64

X_AT = 2 * HOPS
OWN_AT = X_AT + 4
N_SLOTS = OWN_AT + 2


def kernel(
    n_gx,
    n_gy,
    img_ref,
    txt_ref,
    scale_ref,
    offset_ref,
    loss_ref,
    img_out,
    txt_out,
    buf,
    own_n,
    acc,
    loss_acc,
    stage,
    ring_send,
    ring_recv,
    x_send,
    x_recv,
    local_sem,
    out_sem,
):
    rows_here, width = img_ref.shape
    part = rows_here // CHUNKS
    p, q = lax.axis_index("gx"), lax.axis_index("gy")
    core = lax.rem(q, 2)
    last = n_gy - 1

    def gx(value):
        return lax.rem(value + n_gx, n_gx)

    def device(gx_index, gy_index):
        return (gx_index, gy_index)

    wraps_up = q >= n_gy - 2
    wraps_down = q < 2
    up = device(jnp.where(wraps_up, gx(p + 1), p), jnp.where(wraps_up, core, q + 2))
    down = device(jnp.where(wraps_down, gx(p - 1), p), jnp.where(wraps_down, n_gy - 2 + core, q - 2))
    sibling = device(p, q + 1 - 2 * core)
    ninth_to = device(
        jnp.where(core == 1, jnp.where(q == last, gx(p - 1), p), jnp.where(q == 0, gx(p + 1), p)),
        jnp.where(core == 1, jnp.where(q == last, 0, q + 1), jnp.where(q == 0, last, q - 1)),
    )
    ninth_from = device(
        jnp.where(core == 0, jnp.where(q == 0, gx(p + 1), p), jnp.where(q == last, gx(p - 1), p)),
        jnp.where(core == 0, jnp.where(q == 0, last, q - 1), jnp.where(q == last, 0, q + 1)),
    )

    barrier = pltpu.get_barrier_semaphore()
    for source in (up, down, sibling, ninth_from):
        pl.semaphore_signal(barrier, inc=1, device_id=source, device_id_type=MESH)
    pl.semaphore_wait(barrier, 4)

    def piece(j):
        return pl.ds(pl.multiple_of(j * part, part), part)

    def ring_copy(kind, hop, j, src):
        return pltpu.make_async_remote_copy(
            src_ref=src,
            dst_ref=buf.at[kind * HOPS + hop - 1, piece(j)],
            send_sem=ring_send.at[kind, hop - 1, j],
            recv_sem=ring_recv.at[kind, hop - 1, j],
            device_id=up if kind == TXT else down,
            device_id_type=MESH,
        )

    def x_copy(slot, j, src, target):
        return pltpu.make_async_remote_copy(
            src_ref=src,
            dst_ref=buf.at[X_AT + slot, piece(j)],
            send_sem=x_send.at[slot, j],
            recv_sem=x_recv.at[slot, j],
            device_id=target,
            device_id_type=MESH,
        )

    def ring_at(kind, hop, j):
        return buf.at[kind * HOPS + hop - 1, piece(j)]

    inputs = (txt_ref, img_ref)
    short = core
    for j in range(CHUNKS):
        for kind in (TXT, IMG):
            ring_copy(kind, 1, j, inputs[kind].at[piece(j)]).start()
    own_loads = [
        pltpu.make_async_copy(inputs[kind], buf.at[OWN_AT + kind], local_sem.at[kind])
        for kind in (TXT, IMG)
    ]
    for load in own_loads:
        load.start()
    for j in range(CHUNKS):
        for kind in (TXT, IMG):

            @pl.when(short == kind)
            def _():
                x_copy(0, j, inputs[kind].at[piece(j)], sibling).start()

    scale, offset = scale_ref[0], offset_ref[0]
    acc[...] = jnp.zeros_like(acc)
    loss_acc[...] = jnp.zeros_like(loss_acc)
    for load in own_loads:
        load.wait()

    def unit(raw):
        wide = raw.astype(F32)
        inverse = lax.rsqrt(jnp.sum(wide * wide, axis=-1, keepdims=True) + 1e-06)
        return wide * inverse, inverse

    for kind in (TXT, IMG):

        def normalize_own(i, _):
            at = pl.ds(pl.multiple_of(i * FIN_ROWS, FIN_ROWS), FIN_ROWS)
            own_n[kind, at] = unit(buf[OWN_AT + kind, at])[0].astype(BF16)
            return 0

        lax.fori_loop(0, rows_here // FIN_ROWS, normalize_own, 0)

    def visit(slot, j, kind, own_pair):
        block = unit(buf[slot, piece(j)])[0].astype(BF16)
        scores = lax.dot_general(
            own_n[1 - kind], block, (((1,), (1,)), ((), ())), preferred_element_type=F32
        )
        logits = scale * scores + offset
        same = lax.broadcasted_iota(jnp.int32, logits.shape, 0) == (
            lax.broadcasted_iota(jnp.int32, logits.shape, 1) + j * part
        )
        match = jnp.logical_and(same, own_pair)
        drive = jnp.where(match, -logits, logits)
        small = jnp.exp(-jnp.abs(drive))
        whole = 1.0 / (1.0 + small)
        sigmoid = jnp.where(drive >= 0, whole, small * whole)
        coef = (jnp.where(match, -scale, scale) * sigmoid).astype(BF16)

        @pl.when(kind == TXT)
        def _():
            loss_acc[...] += jnp.maximum(drive, 0.0) + jnp.log1p(small)

        acc[kind] += jnp.dot(coef, block, preferred_element_type=F32)

    def finish(kind):
        def some_rows(i, _):
            at = pl.ds(pl.multiple_of(i * FIN_ROWS, FIN_ROWS), FIN_ROWS)
            direction = acc[kind, at]
            u, inverse = unit(buf[OWN_AT + 1 - kind, at])
            grad = inverse * (direction - u * jnp.sum(u * direction, axis=-1, keepdims=True))
            stage[kind, at] = grad.astype(BF16)
            return 0

        lax.fori_loop(0, rows_here // FIN_ROWS, some_rows, 0)
        for one, out in ((TXT, img_out), (IMG, txt_out)):

            @pl.when(kind == one)
            def _():
                pltpu.make_async_copy(stage.at[one], out, out_sem.at[one]).start()

    def step(s, _):
        def chunk(j, _):
            @pl.when(jnp.logical_and(s >= 1, s <= HOPS))
            def _():
                for kind in (TXT, IMG):
                    ring_copy(kind, s, j, ring_at(kind, s, j)).wait_recv()

                    @pl.when(s < HOPS)
                    def _():
                        ring_copy(kind, s + 1, j, ring_at(kind, s, j)).start()

                    @pl.when(jnp.logical_and(s == HOPS, short != kind))
                    def _():
                        x_copy(3, j, ring_at(kind, s, j), ninth_to).start()

                    @pl.when(jnp.logical_and(s == HOPS, short == kind))
                    def _():
                        x_copy(1, j, ring_at(kind, s, j), sibling).start()

                    @pl.when(jnp.logical_and(s == 1, short != kind))
                    def _():
                        x_copy(2, j, ring_at(kind, s, j), sibling).start()

            @pl.when(jnp.logical_and(s == HOPS + 1, j == 0))
            def _():
                finish(1 - core)

            n_visits = jnp.where(
                s == 0, 2, jnp.where(s == HOPS, 3, jnp.where(jnp.logical_or(s <= 2, s > HOPS), 1, 0))
            )

            def one(v, _):
                from_x = jnp.logical_or(jnp.logical_and(s >= 1, s != HOPS), v == 2)
                x_slot = jnp.where(s == 1, 0, jnp.where(s == 2, 2, jnp.where(s == HOPS, 1, 3)))

                @pl.when(from_x)
                def _():
                    x_copy(x_slot, j, buf.at[X_AT, piece(j)], sibling).wait_recv()

                slot = jnp.where(
                    s == 0, OWN_AT + v, jnp.where(from_x, X_AT + x_slot, v * HOPS + HOPS - 1)
                )
                x_kind = jnp.where(jnp.logical_or(s == 1, s == HOPS), 1 - core, core)
                visit(slot, j, jnp.where(from_x, x_kind, v), s == 0)
                return 0

            lax.fori_loop(0, n_visits, one, 0)
            return 0

        lax.fori_loop(0, CHUNKS, chunk, 0)
        return 0

    lax.fori_loop(0, HOPS + 2, step, 0)
    finish(core)
    loss_ref[...] = jnp.sum(loss_acc[...].T, axis=0, keepdims=True) / (4.0 * rows_here)

    def drain(j, _):
        def hop(s, _):
            for kind in (TXT, IMG):
                ring_copy(kind, s, j, ring_at(kind, s, j)).wait_send()
            return 0

        lax.fori_loop(1, HOPS + 1, hop, 0)
        for slot in range(4):
            x_copy(slot, j, buf.at[X_AT, piece(j)], sibling).wait_send()
        return 0

    lax.fori_loop(0, CHUNKS, drain, 0)
    for one, out in ((TXT, img_out), (IMG, txt_out)):
        pltpu.make_async_copy(stage.at[one], out, out_sem.at[one]).wait()


def solution(mesh):
    n_gx, n_gy = mesh.shape["gx"], mesh.shape["gy"]

    def body(img, txt, scale, offset):
        rows, width = img.shape
        part = rows // CHUNKS

        def run(*refs):
            kernel(n_gx, n_gy, *refs)

        any_space = pl.BlockSpec(memory_space=pl.ANY)
        smem = pl.BlockSpec(memory_space=pltpu.SMEM)
        loss, img_grad, txt_grad = pl.pallas_call(
            run,
            out_shape=(
                jax.ShapeDtypeStruct((1, rows), F32),
                jax.ShapeDtypeStruct((rows, width), BF16),
                jax.ShapeDtypeStruct((rows, width), BF16),
            ),
            in_specs=[any_space, any_space, smem, smem],
            out_specs=(pl.BlockSpec(memory_space=pltpu.VMEM), any_space, any_space),
            scratch_shapes=[
                pltpu.VMEM((N_SLOTS, rows, width), BF16),
                pltpu.VMEM((2, rows, width), BF16),
                pltpu.VMEM((2, rows, width), F32),
                pltpu.VMEM((rows, part), F32),
                pltpu.VMEM((2, rows, width), BF16),
                pltpu.SemaphoreType.DMA((2, HOPS, CHUNKS)),
                pltpu.SemaphoreType.DMA((2, HOPS, CHUNKS)),
                pltpu.SemaphoreType.DMA((4, CHUNKS)),
                pltpu.SemaphoreType.DMA((4, CHUNKS)),
                pltpu.SemaphoreType.DMA((2,)),
                pltpu.SemaphoreType.DMA((2,)),
            ],
            compiler_params=pltpu.CompilerParams(
                collective_id=0, has_side_effects=True, vmem_limit_bytes=56 * 1024 * 1024
            ),
            cost_estimate=pl.CostEstimate(
                flops=14 * 2 * rows * rows * width, bytes_accessed=8 * rows * width, transcendentals=0
            ),
        )(img, txt, scale, offset)
        return loss.reshape(rows), img_grad, txt_grad

    return jax.shard_map(
        body,
        mesh=mesh,
        in_specs=(P(("gx", "gy"), None), P(("gx", "gy"), None), P(), P()),
        out_specs=(P(("gx", "gy")), P(("gx", "gy"), None), P(("gx", "gy"), None)),
        check_vma=False,
    )
```

```python
import jax
import jax.numpy as jnp
from jax import lax
from jax.experimental import pallas as pl
from jax.experimental.pallas import tpu as pltpu
from jax.sharding import PartitionSpec as P

MESH = pl.DeviceIdType.MESH
F32 = jnp.float32
BF16 = jnp.bfloat16

TXT, IMG = 0, 1
HOPS = 8
CHUNKS = 4
IN_FLIGHT = 2
FIN_ROWS = 64

X_AT = 2 * HOPS
OWN_AT = X_AT + 4
N_SLOTS = OWN_AT + 2


def kernel(
    n_gx,
    n_gy,
    img_ref,
    txt_ref,
    scale_ref,
    offset_ref,
    grads_ref,
    loss_ref,
    buf,
    own_n,
    acc,
    loss_acc,
    ring_send,
    ring_recv,
    x_send,
    x_recv,
    local_sem,
):
    rows_here, width = img_ref.shape
    part = rows_here // CHUNKS
    p, q = lax.axis_index("gx"), lax.axis_index("gy")
    core = lax.rem(q, 2)
    last = n_gy - 1

    def gx(value):
        return lax.rem(value + n_gx, n_gx)

    def device(gx_index, gy_index):
        return (gx_index, gy_index)

    wraps_up = q >= n_gy - 2
    wraps_down = q < 2
    up = device(jnp.where(wraps_up, gx(p + 1), p), jnp.where(wraps_up, core, q + 2))
    down = device(jnp.where(wraps_down, gx(p - 1), p), jnp.where(wraps_down, n_gy - 2 + core, q - 2))
    sibling = device(p, q + 1 - 2 * core)
    ninth_to = device(
        jnp.where(core == 1, jnp.where(q == last, gx(p - 1), p), jnp.where(q == 0, gx(p + 1), p)),
        jnp.where(core == 1, jnp.where(q == last, 0, q + 1), jnp.where(q == 0, last, q - 1)),
    )
    ninth_from = device(
        jnp.where(core == 0, jnp.where(q == 0, gx(p + 1), p), jnp.where(q == last, gx(p - 1), p)),
        jnp.where(core == 0, jnp.where(q == 0, last, q - 1), jnp.where(q == last, 0, q + 1)),
    )

    barrier = pltpu.get_barrier_semaphore()
    for source in (up, down, sibling, ninth_from):
        pl.semaphore_signal(barrier, inc=1, device_id=source, device_id_type=MESH)
    pl.semaphore_wait(barrier, 4)

    def piece(j):
        return pl.ds(pl.multiple_of(j * part, part), part)

    def ring_copy(kind, hop, j, src):
        return pltpu.make_async_remote_copy(
            src_ref=src,
            dst_ref=buf.at[kind * HOPS + hop - 1, piece(j)],
            send_sem=ring_send.at[kind, hop - 1, j],
            recv_sem=ring_recv.at[kind, hop - 1, j],
            device_id=up if kind == TXT else down,
            device_id_type=MESH,
        )

    def x_copy(slot, j, src, target):
        return pltpu.make_async_remote_copy(
            src_ref=src,
            dst_ref=buf.at[X_AT + slot, piece(j)],
            send_sem=x_send.at[slot, j],
            recv_sem=x_recv.at[slot, j],
            device_id=target,
            device_id_type=MESH,
        )

    def ring_at(kind, hop, j):
        return buf.at[kind * HOPS + hop - 1, piece(j)]

    inputs = (txt_ref, img_ref)
    short = core
    for kind in (TXT, IMG):
        ring_copy(kind, 1, 0, inputs[kind].at[piece(0)]).start()
    own_loads = [
        pltpu.make_async_copy(inputs[kind], buf.at[OWN_AT + kind], local_sem.at[kind])
        for kind in (TXT, IMG)
    ]
    for load in own_loads:
        load.start()
    scale, offset = scale_ref[0], offset_ref[0]
    acc[...] = jnp.zeros_like(acc)
    loss_acc[...] = jnp.zeros_like(loss_acc)
    for load in own_loads:
        load.wait()

    def unit(raw):
        wide = raw.astype(F32)
        inverse = lax.rsqrt(jnp.sum(wide * wide, axis=-1, keepdims=True) + 1e-06)
        return wide * inverse, inverse

    for kind in (TXT, IMG):

        def normalize_own(i, _):
            at = pl.ds(pl.multiple_of(i * FIN_ROWS, FIN_ROWS), FIN_ROWS)
            own_n[kind, at] = unit(buf[OWN_AT + kind, at])[0].astype(BF16)
            return 0

        lax.fori_loop(0, rows_here // FIN_ROWS, normalize_own, 0)

    def visit(slot, j, kind, own_pair):
        block = unit(buf[slot, piece(j)])[0].astype(BF16)
        scores = lax.dot_general(
            own_n[1 - kind], block, (((1,), (1,)), ((), ())), preferred_element_type=F32
        )
        logits = scale * scores + offset
        same = lax.broadcasted_iota(jnp.int32, logits.shape, 0) == (
            lax.broadcasted_iota(jnp.int32, logits.shape, 1) + j * part
        )
        match = jnp.logical_and(same, own_pair)
        drive = jnp.where(match, -logits, logits)
        small = jnp.exp(-jnp.abs(drive))
        whole = 1.0 / (1.0 + small)
        sigmoid = jnp.where(drive >= 0, whole, small * whole)
        coef = (jnp.where(match, -scale, scale) * sigmoid).astype(BF16)

        @pl.when(kind == TXT)
        def _():
            loss_acc[...] += jnp.maximum(drive, 0.0) + jnp.log1p(small)

        acc[kind] += jnp.dot(coef, block, preferred_element_type=F32)

    def finish(kind):
        def some_rows(i, _):
            at = pl.ds(pl.multiple_of(i * FIN_ROWS, FIN_ROWS), FIN_ROWS)
            direction = acc[kind, at]
            u, inverse = unit(buf[OWN_AT + 1 - kind, at])
            grad = inverse * (direction - u * jnp.sum(u * direction, axis=-1, keepdims=True))
            grads_ref[kind, at] = grad.astype(BF16)
            return 0

        lax.fori_loop(0, rows_here // FIN_ROWS, some_rows, 0)

    sends = HOPS * CHUNKS
    tail = sends - 2
    extra = sends + CHUNKS

    def within(i, low, count):
        return jnp.logical_and(i >= low, i < low + count)

    def turn(i, _):
        s, j = lax.div(i, CHUNKS), lax.rem(i, CHUNKS)
        before = jnp.maximum(i - IN_FLIGHT, 0)
        for kind in (TXT, IMG):

            @pl.when(within(i, IN_FLIGHT, sends))
            def _():
                at = lax.rem(before, CHUNKS)
                ring_copy(kind, lax.div(before, CHUNKS) + 1, at, ring_at(kind, 1, at)).wait_send()

            @pl.when(jnp.logical_and(within(i, sends + IN_FLIGHT, CHUNKS), short != kind))
            def _():
                at = lax.rem(before, CHUNKS)
                x_copy(3, at, ring_at(kind, HOPS, at), ninth_to).wait_send()

            @pl.when(within(i, 1, CHUNKS - 1))
            def _():
                ring_copy(kind, 1, j, inputs[kind].at[piece(j)]).start()

            @pl.when(within(i, CHUNKS, sends - CHUNKS))
            def _():
                ring_copy(kind, s, j, ring_at(kind, s, j)).wait_recv()
                ring_copy(kind, s + 1, j, ring_at(kind, s, j)).start()

            @pl.when(jnp.logical_and(within(i, sends, CHUNKS), short != kind))
            def _():
                x_copy(3, j, ring_at(kind, HOPS, j), ninth_to).start()

            @pl.when(jnp.logical_and(within(i, 0, CHUNKS), short == kind))
            def _():
                x_copy(0, j, inputs[kind].at[piece(j)], sibling).start()

            @pl.when(jnp.logical_and(within(i, CHUNKS, CHUNKS), short != kind))
            def _():
                x_copy(2, j, ring_at(kind, 1, j), sibling).start()

            @pl.when(within(i, tail, CHUNKS))
            def _():
                at = i - tail
                ring_copy(kind, HOPS, at, ring_at(kind, HOPS, at)).wait_recv()

                @pl.when(short == kind)
                def _():
                    x_copy(1, at, ring_at(kind, HOPS, at), sibling).start()

        @pl.when(i == extra)
        def _():
            finish(1 - core)

        in_tail = within(i, tail, CHUNKS)
        pairs = jnp.where(jnp.logical_or(i < CHUNKS, in_tail), 2, 0)
        x_early = within(i, CHUNKS, 2 * CHUNKS)
        x_tail = within(i, tail + 1, CHUNKS)
        x_last = i >= extra
        from_x = jnp.where(jnp.logical_or(jnp.logical_or(x_early, x_tail), x_last), 1, 0)
        x_slot = jnp.where(x_last, 3, jnp.where(x_tail, 1, jnp.where(s == 1, 0, 2)))
        x_piece = jnp.where(x_tail, i - tail - 1, j)
        x_kind = jnp.where(x_slot < 2, 1 - core, core)

        def one(v, _):
            is_x = v >= pairs

            @pl.when(is_x)
            def _():
                x_copy(x_slot, x_piece, buf.at[X_AT, piece(x_piece)], sibling).wait_recv()

            slot = jnp.where(
                is_x, X_AT + x_slot, jnp.where(in_tail, v * HOPS + HOPS - 1, OWN_AT + v)
            )
            at = jnp.where(is_x, x_piece, jnp.where(in_tail, i - tail, j))
            visit(slot, at, jnp.where(is_x, x_kind, v), i < CHUNKS)
            return 0

        lax.fori_loop(0, pairs + from_x, one, 0)
        return 0

    lax.fori_loop(0, extra + CHUNKS, turn, 0)
    finish(core)
    loss_ref[...] = jnp.sum(loss_acc[...].T, axis=0, keepdims=True) / (4.0 * rows_here)

    def drain(j, _):
        for slot in range(3):
            x_copy(slot, j, buf.at[X_AT, piece(j)], sibling).wait_send()
        return 0

    lax.fori_loop(0, CHUNKS, drain, 0)


def hand_out(grads_ref, loss_in, img_out, txt_out, loss_out, sems):
    copies = [
        pltpu.make_async_copy(grads_ref.at[one], out, sems.at[one])
        for one, out in ((TXT, img_out), (IMG, txt_out))
    ]
    for copy in copies:
        copy.start()
    loss_out[...] = loss_in[...]
    for copy in copies:
        copy.wait()


def solution(mesh):
    n_gx, n_gy = mesh.shape["gx"], mesh.shape["gy"]

    def body(img, txt, scale, offset):
        rows, width = img.shape
        part = rows // CHUNKS

        def run(*refs):
            kernel(n_gx, n_gy, *refs)

        any_space = pl.BlockSpec(memory_space=pl.ANY)
        smem = pl.BlockSpec(memory_space=pltpu.SMEM)
        vmem = pl.BlockSpec(memory_space=pltpu.VMEM)
        grads, loss = pl.pallas_call(
            run,
            out_shape=(pltpu.VMEM((2, rows, width), BF16), pltpu.VMEM((1, rows), F32)),
            in_specs=[any_space, any_space, smem, smem],
            out_specs=(vmem, vmem),
            scratch_shapes=[
                pltpu.VMEM((N_SLOTS, rows, width), BF16),
                pltpu.VMEM((2, rows, width), BF16),
                pltpu.VMEM((2, rows, width), F32),
                pltpu.VMEM((rows, part), F32),
                pltpu.SemaphoreType.DMA((2, HOPS, CHUNKS)),
                pltpu.SemaphoreType.DMA((2, HOPS, CHUNKS)),
                pltpu.SemaphoreType.DMA((4, CHUNKS)),
                pltpu.SemaphoreType.DMA((4, CHUNKS)),
                pltpu.SemaphoreType.DMA((2,)),
            ],
            compiler_params=pltpu.CompilerParams(
                collective_id=0, has_side_effects=True, vmem_limit_bytes=52 * 1024 * 1024
            ),
            cost_estimate=pl.CostEstimate(
                flops=14 * 2 * rows * rows * width, bytes_accessed=8 * rows * width, transcendentals=0
            ),
        )(img, txt, scale, offset)
        img_grad, txt_grad, loss = pl.pallas_call(
            hand_out,
            out_shape=(
                jax.ShapeDtypeStruct((rows, width), BF16),
                jax.ShapeDtypeStruct((rows, width), BF16),
                jax.ShapeDtypeStruct((1, rows), F32),
            ),
            in_specs=[vmem, vmem],
            out_specs=(any_space, any_space, vmem),
            scratch_shapes=[pltpu.SemaphoreType.DMA((2,))],
        )(grads, loss)
        return loss.reshape(rows), img_grad, txt_grad

    return jax.shard_map(
        body,
        mesh=mesh,
        in_specs=(P(("gx", "gy"), None), P(("gx", "gy"), None), P(), P()),
        out_specs=(P(("gx", "gy")), P(("gx", "gy"), None), P(("gx", "gy"), None)),
        check_vma=False,
    )
```

```python
import jax
import jax.numpy as jnp
from jax import lax
from jax.experimental import pallas as pl
from jax.experimental.pallas import tpu as pltpu
from jax.sharding import PartitionSpec as P

MESH = pl.DeviceIdType.MESH
F32 = jnp.float32
BF16 = jnp.bfloat16

TXT, IMG = 0, 1
HOPS = 8
PIECES = 4
HALVES = 2
SEMS = 16
SUB = 64
FIN_ROWS = 32

X_AT = 2 * HOPS
OWN_AT = X_AT + 4
N_SLOTS = OWN_AT + 2


def kernel(
    n_gx,
    n_gy,
    img_ref,
    txt_ref,
    scale_ref,
    offset_ref,
    grads_ref,
    loss_ref,
    buf,
    own_n,
    acc,
    loss_acc,
    block,
    scores,
    coef,
    ring_send,
    ring_recv,
    x_send,
    x_recv,
    local_sem,
):
    rows_here, width = img_ref.shape
    part, half = rows_here // PIECES, rows_here // HALVES
    sends = HOPS * PIECES
    p, q = lax.axis_index("gx"), lax.axis_index("gy")
    core = lax.rem(q, 2)
    last = n_gy - 1

    def gx(value):
        return lax.rem(value + n_gx, n_gx)

    def device(gx_index, gy_index):
        return (gx_index, gy_index)

    wraps_up = q >= n_gy - 2
    wraps_down = q < 2
    up = device(jnp.where(wraps_up, gx(p + 1), p), jnp.where(wraps_up, core, q + 2))
    down = device(jnp.where(wraps_down, gx(p - 1), p), jnp.where(wraps_down, n_gy - 2 + core, q - 2))
    sibling = device(p, q + 1 - 2 * core)
    ninth_to = device(
        jnp.where(core == 1, jnp.where(q == last, gx(p - 1), p), jnp.where(q == 0, gx(p + 1), p)),
        jnp.where(core == 1, jnp.where(q == last, 0, q + 1), jnp.where(q == 0, last, q - 1)),
    )
    ninth_from = device(
        jnp.where(core == 0, jnp.where(q == 0, gx(p + 1), p), jnp.where(q == last, gx(p - 1), p)),
        jnp.where(core == 0, jnp.where(q == 0, last, q - 1), jnp.where(q == last, 0, q + 1)),
    )

    barrier = pltpu.get_barrier_semaphore()
    for source in (up, down, sibling, ninth_from):
        pl.semaphore_signal(barrier, inc=1, device_id=source, device_id_type=MESH)
    pl.semaphore_wait(barrier, 4)

    def piece(j):
        return pl.ds(pl.multiple_of(j * part, part), part)

    def half_of(h):
        return pl.ds(pl.multiple_of(h * half, half), half)

    def landing(kind, n):
        return buf.at[kind * HOPS + lax.div(n, PIECES), piece(lax.rem(n, PIECES))]

    def ring_copy(kind, n, src):
        return pltpu.make_async_remote_copy(
            src_ref=src,
            dst_ref=landing(kind, n),
            send_sem=ring_send.at[kind, lax.rem(n, SEMS)],
            recv_sem=ring_recv.at[kind, n],
            device_id=up if kind == TXT else down,
            device_id_type=MESH,
        )

    def x_copy(slot, j, src, target):
        return pltpu.make_async_remote_copy(
            src_ref=src,
            dst_ref=buf.at[X_AT + slot, piece(j)],
            send_sem=x_send.at[slot, j],
            recv_sem=x_recv.at[slot, j],
            device_id=target,
            device_id_type=MESH,
        )

    inputs = (txt_ref, img_ref)
    short = core

    def set_out(n):
        n = jnp.int32(n)
        for kind in (TXT, IMG):
            ring_copy(kind, n, inputs[kind].at[piece(n)]).start()

    def unit(raw):
        wide = raw.astype(F32)
        return wide * lax.rsqrt(jnp.sum(wide * wide, axis=-1, keepdims=True) + 1e-06)

    def normalize_own(kind):
        def some_rows(i, _):
            at = pl.ds(pl.multiple_of(i * FIN_ROWS, FIN_ROWS), FIN_ROWS)
            own_n[kind, at] = unit(buf[OWN_AT + kind, at]).astype(BF16)
            return 0

        lax.fori_loop(0, rows_here // FIN_ROWS, some_rows, 0)

    set_out(0)
    own_loads = [
        pltpu.make_async_copy(inputs[kind], buf.at[OWN_AT + kind], local_sem.at[kind])
        for kind in (TXT, IMG)
    ]
    for load in own_loads:
        load.start()
    scale, offset = scale_ref[0], offset_ref[0]
    acc[...] = jnp.zeros_like(acc)
    loss_acc[...] = jnp.zeros_like(loss_acc)
    set_out(1)
    for load in own_loads:
        load.wait()
    normalize_own(TXT)
    set_out(2)
    normalize_own(IMG)
    set_out(3)

    def weigh(h, own_pair, with_loss):
        def some_rows(i, _):
            at = pl.ds(pl.multiple_of(i * SUB, SUB), SUB)
            drive = scale * scores[at] + offset
            weight = scale
            if own_pair:
                row = lax.broadcasted_iota(jnp.int32, drive.shape, 0) + i * SUB
                match = row == lax.broadcasted_iota(jnp.int32, drive.shape, 1) + h * half
                drive = jnp.where(match, -drive, drive)
                weight = jnp.where(match, -scale, scale)
            power = jnp.exp(drive)
            coef[at] = (weight * (power * (1.0 / (1.0 + power)))).astype(BF16)
            if with_loss:
                loss = jnp.log1p(power)
                fold = half // 2
                loss_acc[at] += loss[:, :fold] + loss[:, fold:]
            return 0

        lax.fori_loop(0, rows_here // SUB, some_rows, 0, unroll=2)

    def visit(slot, h, kind, own_pair):
        def some_rows(i, _):
            at = pl.ds(pl.multiple_of(h * half + i * FIN_ROWS, FIN_ROWS), FIN_ROWS)
            to = pl.ds(pl.multiple_of(i * FIN_ROWS, FIN_ROWS), FIN_ROWS)
            block[to] = unit(buf[slot, at]).astype(BF16)
            return 0

        lax.fori_loop(0, half // FIN_ROWS, some_rows, 0, unroll=4)
        for r in range(HALVES):
            at = pl.ds(r * half, half)
            scores[at] = lax.dot_general(
                own_n[1 - kind, at], block[...], (((1,), (1,)), ((), ())), preferred_element_type=F32
            )
        for one in (TXT, IMG):

            @pl.when(jnp.logical_and(own_pair, kind == one))
            def _():
                weigh(h, True, one == TXT)

            @pl.when(jnp.logical_and(jnp.logical_not(own_pair), kind == one))
            def _():
                weigh(h, False, one == TXT)

        for r in range(HALVES):
            at = pl.ds(r * half, half)
            acc[kind, at] += jnp.dot(coef[at], block[...], preferred_element_type=F32)

    def finish(kind):
        def some_rows(i, _):
            at = pl.ds(pl.multiple_of(i * FIN_ROWS, FIN_ROWS), FIN_ROWS)
            direction = acc[kind, at]
            raw = buf[OWN_AT + 1 - kind, at].astype(F32)
            inverse = lax.rsqrt(jnp.sum(raw * raw, axis=-1, keepdims=True) + 1e-06)
            along = jnp.sum(raw * direction, axis=-1, keepdims=True) * (inverse * inverse * inverse)
            grads_ref[kind, at] = (inverse * direction - along * raw).astype(BF16)
            return 0

        lax.fori_loop(0, rows_here // FIN_ROWS, some_rows, 0, unroll=4)

    def within(i, low, count):
        return jnp.logical_and(i >= low, i < low + count)

    ending = sends - 3

    def turn(i, _):
        t = jnp.where(i > ending, i - 1, i)

        @pl.when(jnp.logical_and(t < sends, i != ending + 1))
        def _():
            onward = t + PIECES
            j = lax.rem(t, PIECES)
            for kind in (TXT, IMG):
                ring_copy(kind, t, landing(kind, t)).wait_recv()

                @pl.when(onward < sends)
                def _():
                    ring_copy(kind, onward, landing(kind, t)).start()

                @pl.when(jnp.logical_and(onward >= sends, short != kind))
                def _():
                    x_copy(3, j, landing(kind, t), ninth_to).start()

                @pl.when(jnp.logical_and(onward >= sends, short == kind))
                def _():
                    x_copy(1, j, landing(kind, t), sibling).start()

                @pl.when(jnp.logical_and(t < PIECES, short != kind))
                def _():
                    x_copy(2, j, landing(kind, t), sibling).start()

                @pl.when(jnp.logical_and(t < PIECES, short == kind))
                def _():
                    x_copy(0, j, inputs[kind].at[piece(j)], sibling).start()

                @pl.when(t >= PIECES)
                def _():
                    ring_copy(kind, t - PIECES, landing(kind, t)).wait_send()

        since = i - ending

        @pl.when(since == 7)
        def _():
            finish(1 - core)

        is_end = since >= 0
        is_own = i < 4
        is_x_early = within(i, 4, 4)
        step = lax.rem(jnp.maximum(since, 0), 3)
        is_x3 = since >= 6
        is_x1 = jnp.logical_and(within(since, 0, 6), step == 2)
        is_x = jnp.logical_or(is_x_early, jnp.logical_or(is_x1, is_x3))
        x_slot = jnp.where(is_x3, 3, jnp.where(is_x1, 1, jnp.where(i < 6, 0, 2)))
        kind = jnp.where(
            is_x, jnp.where(x_slot < 2, 1 - core, core), jnp.where(is_end, step, lax.rem(i, 2))
        )
        slot = jnp.where(
            is_x, X_AT + x_slot, jnp.where(is_end, kind * HOPS + HOPS - 1, OWN_AT + kind)
        )
        h = jnp.where(
            is_end,
            jnp.where(is_x3, since - 6, jnp.where(since >= 3, 1, 0)),
            jnp.where(is_own, lax.div(i, 2), lax.rem(i, 2)),
        )

        @pl.when(is_x)
        def _():
            for k in range(PIECES // HALVES):
                j = h * (PIECES // HALVES) + k
                x_copy(x_slot, j, buf.at[X_AT, piece(j)], sibling).wait_recv()

        @pl.when(jnp.logical_or(is_end, i < 8))
        def _():
            visit(slot, h, kind, is_own)

        return 0

    lax.fori_loop(0, ending + 8, turn, 0)
    finish(core)
    loss_ref[...] = jnp.sum(loss_acc[...].T, axis=0, keepdims=True) / (4.0 * rows_here)

    def drain(j, _):
        for slot in range(4):
            x_copy(slot, j, buf.at[X_AT, piece(j)], sibling).wait_send()
        for kind in (TXT, IMG):
            n = sends - PIECES + j
            ring_copy(kind, n, landing(kind, n)).wait_send()
        return 0

    lax.fori_loop(0, PIECES, drain, 0)


def hand_out(grads_ref, loss_in, img_out, txt_out, loss_out, sems):
    copies = [
        pltpu.make_async_copy(grads_ref.at[one], out, sems.at[one])
        for one, out in ((TXT, img_out), (IMG, txt_out))
    ]
    for copy in copies:
        copy.start()
    loss_out[...] = loss_in[...]
    for copy in copies:
        copy.wait()


def solution(mesh):
    n_gx, n_gy = mesh.shape["gx"], mesh.shape["gy"]

    def body(img, txt, scale, offset):
        rows, width = img.shape
        half = rows // HALVES
        sends = HOPS * PIECES

        def run(*refs):
            kernel(n_gx, n_gy, *refs)

        any_space = pl.BlockSpec(memory_space=pl.ANY)
        smem = pl.BlockSpec(memory_space=pltpu.SMEM)
        vmem = pl.BlockSpec(memory_space=pltpu.VMEM)
        grads, loss = pl.pallas_call(
            run,
            out_shape=(pltpu.VMEM((2, rows, width), BF16), pltpu.VMEM((1, rows), F32)),
            in_specs=[any_space, any_space, smem, smem],
            out_specs=(vmem, vmem),
            scratch_shapes=[
                pltpu.VMEM((N_SLOTS, rows, width), BF16),
                pltpu.VMEM((2, rows, width), BF16),
                pltpu.VMEM((2, rows, width), F32),
                pltpu.VMEM((rows, half // 2), F32),
                pltpu.VMEM((half, width), BF16),
                pltpu.VMEM((rows, half), F32),
                pltpu.VMEM((rows, half), BF16),
                pltpu.SemaphoreType.DMA((2, SEMS)),
                pltpu.SemaphoreType.DMA((2, sends)),
                pltpu.SemaphoreType.DMA((4, PIECES)),
                pltpu.SemaphoreType.DMA((4, PIECES)),
                pltpu.SemaphoreType.DMA((2,)),
            ],
            compiler_params=pltpu.CompilerParams(
                collective_id=0, has_side_effects=True, vmem_limit_bytes=52 * 1024 * 1024
            ),
            cost_estimate=pl.CostEstimate(
                flops=14 * 2 * rows * rows * width, bytes_accessed=8 * rows * width, transcendentals=0
            ),
        )(img, txt, scale, offset)
        img_grad, txt_grad, loss = pl.pallas_call(
            hand_out,
            out_shape=(
                jax.ShapeDtypeStruct((rows, width), BF16),
                jax.ShapeDtypeStruct((rows, width), BF16),
                jax.ShapeDtypeStruct((1, rows), F32),
            ),
            in_specs=[vmem, vmem],
            out_specs=(any_space, any_space, vmem),
            scratch_shapes=[pltpu.SemaphoreType.DMA((2,))],
            compiler_params=pltpu.CompilerParams(vmem_limit_bytes=4 * 1024 * 1024),
        )(grads, loss)
        return loss.reshape(rows), img_grad, txt_grad

    return jax.shard_map(
        body,
        mesh=mesh,
        in_specs=(P(("gx", "gy"), None), P(("gx", "gy"), None), P(), P()),
        out_specs=(P(("gx", "gy")), P(("gx", "gy"), None), P(("gx", "gy"), None)),
        check_vma=False,
    )
```

```python
import jax
import jax.numpy as jnp
from jax import lax
from jax.experimental import pallas as pl
from jax.experimental.pallas import tpu as pltpu
from jax.sharding import PartitionSpec as P

MESH = pl.DeviceIdType.MESH
F32 = jnp.float32
BF16 = jnp.bfloat16

TXT, IMG = 0, 1
HOPS = 8
PIECES = 4
HALVES = 2
SEMS = 16
SUB = 64
FIN_ROWS = 32

X_AT = 2 * HOPS
OWN_AT = X_AT + 4
N_SLOTS = OWN_AT + 2


def kernel(
    n_gx,
    n_gy,
    img_ref,
    txt_ref,
    scale_ref,
    offset_ref,
    grads_ref,
    loss_ref,
    buf,
    own_n,
    acc,
    loss_acc,
    block,
    scores,
    coef,
    own_inv,
    ring_send,
    ring_recv,
    x_send,
    x_recv,
    local_sem,
):
    rows_here, width = img_ref.shape
    part, half = rows_here // PIECES, rows_here // HALVES
    sends = HOPS * PIECES
    p, q = lax.axis_index("gx"), lax.axis_index("gy")
    core = lax.rem(q, 2)
    last = n_gy - 1

    def gx(value):
        return lax.rem(value + n_gx, n_gx)

    def device(gx_index, gy_index):
        return (gx_index, gy_index)

    wraps_up = q >= n_gy - 2
    wraps_down = q < 2
    up = device(jnp.where(wraps_up, gx(p + 1), p), jnp.where(wraps_up, core, q + 2))
    down = device(jnp.where(wraps_down, gx(p - 1), p), jnp.where(wraps_down, n_gy - 2 + core, q - 2))
    sibling = device(p, q + 1 - 2 * core)
    ninth_to = device(
        jnp.where(core == 1, jnp.where(q == last, gx(p - 1), p), jnp.where(q == 0, gx(p + 1), p)),
        jnp.where(core == 1, jnp.where(q == last, 0, q + 1), jnp.where(q == 0, last, q - 1)),
    )
    ninth_from = device(
        jnp.where(core == 0, jnp.where(q == 0, gx(p + 1), p), jnp.where(q == last, gx(p - 1), p)),
        jnp.where(core == 0, jnp.where(q == 0, last, q - 1), jnp.where(q == last, 0, q + 1)),
    )

    barrier = pltpu.get_barrier_semaphore()
    for source in (up, down, sibling, ninth_from):
        pl.semaphore_signal(barrier, inc=1, device_id=source, device_id_type=MESH)
    pl.semaphore_wait(barrier, 4)

    def piece(j):
        return pl.ds(pl.multiple_of(j * part, part), part)

    def half_of(h):
        return pl.ds(pl.multiple_of(h * half, half), half)

    def landing(kind, n):
        return buf.at[kind * HOPS + lax.div(n, PIECES), piece(lax.rem(n, PIECES))]

    def ring_copy(kind, n, src):
        return pltpu.make_async_remote_copy(
            src_ref=src,
            dst_ref=landing(kind, n),
            send_sem=ring_send.at[kind, lax.rem(n, SEMS)],
            recv_sem=ring_recv.at[kind, n],
            device_id=up if kind == TXT else down,
            device_id_type=MESH,
        )

    def x_copy(slot, j, src, target):
        return pltpu.make_async_remote_copy(
            src_ref=src,
            dst_ref=buf.at[X_AT + slot, piece(j)],
            send_sem=x_send.at[slot, j],
            recv_sem=x_recv.at[slot, j],
            device_id=target,
            device_id_type=MESH,
        )

    inputs = (txt_ref, img_ref)
    short = core

    def set_out(n):
        n = jnp.int32(n)
        for kind in (TXT, IMG):
            ring_copy(kind, n, inputs[kind].at[piece(n)]).start()

    def inverse_of(wide):
        return lax.rsqrt(jnp.sum(wide * wide, axis=-1, keepdims=True) + 1e-06)

    def normalize_own(kind):
        def some_rows(i, _):
            at = pl.ds(pl.multiple_of(i * FIN_ROWS, FIN_ROWS), FIN_ROWS)
            wide = buf[OWN_AT + kind, at].astype(F32)
            inverse = inverse_of(wide)
            own_inv[kind, at] = inverse
            own_n[kind, at] = (wide * inverse).astype(BF16)
            return 0

        lax.fori_loop(0, rows_here // FIN_ROWS, some_rows, 0, unroll=4)

    set_out(0)
    own_loads = [
        pltpu.make_async_copy(inputs[kind], buf.at[OWN_AT + kind], local_sem.at[kind])
        for kind in (TXT, IMG)
    ]
    for load in own_loads:
        load.start()
    acc[...] = jnp.zeros_like(acc)
    loss_acc[...] = jnp.zeros_like(loss_acc)
    set_out(1)
    for load in own_loads:
        load.wait()
    scale, offset = scale_ref[0], offset_ref[0]
    normalize_own(TXT)
    set_out(2)
    normalize_own(IMG)
    set_out(3)

    def weigh(h, own_pair, with_loss):
        def some_rows(i, _):
            at = pl.ds(pl.multiple_of(i * SUB, SUB), SUB)
            drive = scale * scores[at] + offset
            weight = scale
            if own_pair:
                row = lax.broadcasted_iota(jnp.int32, drive.shape, 0) + i * SUB
                match = row == lax.broadcasted_iota(jnp.int32, drive.shape, 1) + h * half
                drive = jnp.where(match, -drive, drive)
                weight = jnp.where(match, -scale, scale)
            power = jnp.exp(drive)
            whole = 1.0 + power
            rough = pl.reciprocal(whole, approx=True)
            coef[at] = (weight * power * (rough * (2.0 - whole * rough))).astype(BF16)
            if with_loss:
                loss = jnp.log(whole)
                fold = half // 2
                loss_acc[at] += loss[:, :fold] + loss[:, fold:]
            return 0

        lax.fori_loop(0, rows_here // SUB, some_rows, 0, unroll=2)

    def visit(slot, h, kind, own_pair):
        def some_rows(i, _):
            at = pl.ds(pl.multiple_of(h * half + i * FIN_ROWS, FIN_ROWS), FIN_ROWS)
            to = pl.ds(pl.multiple_of(i * FIN_ROWS, FIN_ROWS), FIN_ROWS)
            wide = buf[slot, at].astype(F32)
            block[to] = (wide * inverse_of(wide)).astype(BF16)
            return 0

        lax.fori_loop(0, half // FIN_ROWS, some_rows, 0, unroll=4)
        for r in range(HALVES):
            at = pl.ds(r * half, half)
            scores[at] = lax.dot_general(
                own_n[1 - kind, at], block[...], (((1,), (1,)), ((), ())), preferred_element_type=F32
            )
        for one in (TXT, IMG):

            @pl.when(jnp.logical_and(own_pair, kind == one))
            def _():
                weigh(h, True, one == TXT)

            @pl.when(jnp.logical_and(jnp.logical_not(own_pair), kind == one))
            def _():
                weigh(h, False, one == TXT)

        for r in range(HALVES):
            at = pl.ds(r * half, half)
            acc[kind, at] += jnp.dot(coef[at], block[...], preferred_element_type=F32)

    def finish(kind):
        def some_rows(i, _):
            at = pl.ds(pl.multiple_of(i * FIN_ROWS, FIN_ROWS), FIN_ROWS)
            direction = acc[kind, at]
            raw = buf[OWN_AT + 1 - kind, at].astype(F32)
            inverse = own_inv[1 - kind, at]
            along = jnp.sum(raw * direction, axis=-1, keepdims=True) * (inverse * inverse * inverse)
            grads_ref[kind, at] = (inverse * direction - along * raw).astype(BF16)
            return 0

        lax.fori_loop(0, rows_here // FIN_ROWS, some_rows, 0, unroll=4)

    def within(i, low, count):
        return jnp.logical_and(i >= low, i < low + count)

    def drain(j, _):
        for slot in range(4):
            x_copy(slot, j, buf.at[X_AT, piece(j)], sibling).wait_send()
        for kind in (TXT, IMG):
            n = sends - PIECES + j
            ring_copy(kind, n, landing(kind, n)).wait_send()
        return 0

    ending = sends - 3

    def turn(i, _):
        t = jnp.where(i > ending, i - 1, i)

        @pl.when(jnp.logical_and(t < sends, i != ending + 1))
        def _():
            onward = t + PIECES
            j = lax.rem(t, PIECES)
            for kind in (TXT, IMG):
                ring_copy(kind, t, landing(kind, t)).wait_recv()

                @pl.when(onward < sends)
                def _():
                    ring_copy(kind, onward, landing(kind, t)).start()

                @pl.when(jnp.logical_and(onward >= sends, short != kind))
                def _():
                    x_copy(3, j, landing(kind, t), ninth_to).start()

                @pl.when(jnp.logical_and(onward >= sends, short == kind))
                def _():
                    x_copy(1, j, landing(kind, t), sibling).start()

                @pl.when(jnp.logical_and(t < PIECES, short != kind))
                def _():
                    x_copy(2, j, landing(kind, t), sibling).start()

                @pl.when(jnp.logical_and(t < PIECES, short == kind))
                def _():
                    x_copy(0, j, inputs[kind].at[piece(j)], sibling).start()

                @pl.when(t >= PIECES)
                def _():
                    ring_copy(kind, t - PIECES, landing(kind, t)).wait_send()

        since = i - ending

        @pl.when(since == 7)
        def _():
            finish(1 - core)
            lax.fori_loop(0, PIECES, drain, 0)

        is_end = since >= 0
        is_own = i < 4
        is_x_early = within(i, 4, 4)
        step = lax.rem(jnp.maximum(since, 0), 3)
        is_x3 = since >= 6
        is_x1 = jnp.logical_and(within(since, 0, 6), step == 2)
        is_x = jnp.logical_or(is_x_early, jnp.logical_or(is_x1, is_x3))
        x_slot = jnp.where(is_x3, 3, jnp.where(is_x1, 1, jnp.where(i < 6, 0, 2)))
        kind = jnp.where(
            is_x, jnp.where(x_slot < 2, 1 - core, core), jnp.where(is_end, step, lax.rem(i, 2))
        )
        slot = jnp.where(
            is_x, X_AT + x_slot, jnp.where(is_end, kind * HOPS + HOPS - 1, OWN_AT + kind)
        )
        h = jnp.where(
            is_end,
            jnp.where(is_x3, since - 6, jnp.where(since >= 3, 1, 0)),
            jnp.where(is_own, lax.div(i, 2), lax.rem(i, 2)),
        )

        @pl.when(is_x)
        def _():
            for k in range(PIECES // HALVES):
                j = h * (PIECES // HALVES) + k
                x_copy(x_slot, j, buf.at[X_AT, piece(j)], sibling).wait_recv()

        @pl.when(jnp.logical_or(is_end, i < 8))
        def _():
            visit(slot, h, kind, is_own)

        return 0

    lax.fori_loop(0, ending + 8, turn, 0)
    finish(core)
    loss_ref[...] = jnp.sum(loss_acc[...].T, axis=0, keepdims=True) / (4.0 * rows_here)


def hand_out(grads_ref, loss_in, img_out, txt_out, loss_out, sems):
    copies = [
        pltpu.make_async_copy(grads_ref.at[one], out, sems.at[one])
        for one, out in ((TXT, img_out), (IMG, txt_out))
    ]
    for copy in copies:
        copy.start()
    loss_out[...] = loss_in[...]
    for copy in copies:
        copy.wait()


def solution(mesh):
    n_gx, n_gy = mesh.shape["gx"], mesh.shape["gy"]

    def body(img, txt, scale, offset):
        rows, width = img.shape
        half = rows // HALVES
        sends = HOPS * PIECES

        def run(*refs):
            kernel(n_gx, n_gy, *refs)

        any_space = pl.BlockSpec(memory_space=pl.ANY)
        smem = pl.BlockSpec(memory_space=pltpu.SMEM)
        vmem = pl.BlockSpec(memory_space=pltpu.VMEM)
        grads, loss = pl.pallas_call(
            run,
            out_shape=(pltpu.VMEM((2, rows, width), BF16), pltpu.VMEM((1, rows), F32)),
            in_specs=[any_space, any_space, smem, smem],
            out_specs=(vmem, vmem),
            scratch_shapes=[
                pltpu.VMEM((N_SLOTS, rows, width), BF16),
                pltpu.VMEM((2, rows, width), BF16),
                pltpu.VMEM((2, rows, width), F32),
                pltpu.VMEM((rows, half // 2), F32),
                pltpu.VMEM((half, width), BF16),
                pltpu.VMEM((rows, half), F32),
                pltpu.VMEM((rows, half), BF16),
                pltpu.VMEM((2, rows, 1), F32),
                pltpu.SemaphoreType.DMA((2, SEMS)),
                pltpu.SemaphoreType.DMA((2, sends)),
                pltpu.SemaphoreType.DMA((4, PIECES)),
                pltpu.SemaphoreType.DMA((4, PIECES)),
                pltpu.SemaphoreType.DMA((2,)),
            ],
            compiler_params=pltpu.CompilerParams(
                collective_id=0, has_side_effects=True, vmem_limit_bytes=52 * 1024 * 1024
            ),
            cost_estimate=pl.CostEstimate(
                flops=14 * 2 * rows * rows * width, bytes_accessed=8 * rows * width, transcendentals=0
            ),
        )(img, txt, scale, offset)
        img_grad, txt_grad, loss = pl.pallas_call(
            hand_out,
            out_shape=(
                jax.ShapeDtypeStruct((rows, width), BF16),
                jax.ShapeDtypeStruct((rows, width), BF16),
                jax.ShapeDtypeStruct((1, rows), F32),
            ),
            in_specs=[vmem, vmem],
            out_specs=(any_space, any_space, vmem),
            scratch_shapes=[pltpu.SemaphoreType.DMA((2,))],
            compiler_params=pltpu.CompilerParams(vmem_limit_bytes=4 * 1024 * 1024),
        )(grads, loss)
        return loss.reshape(rows), img_grad, txt_grad

    return jax.shard_map(
        body,
        mesh=mesh,
        in_specs=(P(("gx", "gy"), None), P(("gx", "gy"), None), P(), P()),
        out_specs=(P(("gx", "gy")), P(("gx", "gy"), None), P(("gx", "gy"), None)),
        check_vma=False,
    )
```

```python
import jax
import jax.numpy as jnp
from jax import lax
from jax.experimental import pallas as pl
from jax.experimental.pallas import tpu as pltpu
from jax.sharding import PartitionSpec as P

MESH = pl.DeviceIdType.MESH
F32 = jnp.float32
BF16 = jnp.bfloat16

TXT, IMG = 0, 1
HOPS = 8
PIECES = 4
OWN_NINTH = 2
HALVES = 2
SEMS = 16
SUB = 64
FIN_ROWS = 32

X_AT = 2 * HOPS
OWN_AT = X_AT + 4
N_SLOTS = OWN_AT + 2


def kernel(
    n_gx,
    n_gy,
    img_ref,
    txt_ref,
    scale_ref,
    offset_ref,
    grads_ref,
    loss_ref,
    buf,
    own_n,
    acc,
    loss_acc,
    block,
    scores,
    coef,
    shared,
    shared_send,
    shared_recv,
    ring_send,
    ring_recv,
    x_send,
    x_recv,
    local_sem,
):
    rows_here, width = img_ref.shape
    part, half = rows_here // PIECES, rows_here // HALVES
    sends = HOPS * PIECES
    p, q = lax.axis_index("gx"), lax.axis_index("gy")
    core = lax.rem(q, 2)
    last = n_gy - 1

    def gx(value):
        return lax.rem(value + n_gx, n_gx)

    def device(gx_index, gy_index):
        return (gx_index, gy_index)

    wraps_up = q >= n_gy - 2
    wraps_down = q < 2
    up = device(jnp.where(wraps_up, gx(p + 1), p), jnp.where(wraps_up, core, q + 2))
    down = device(jnp.where(wraps_down, gx(p - 1), p), jnp.where(wraps_down, n_gy - 2 + core, q - 2))
    sibling = device(p, q + 1 - 2 * core)
    ninth_to = device(
        jnp.where(core == 1, jnp.where(q == last, gx(p - 1), p), jnp.where(q == 0, gx(p + 1), p)),
        jnp.where(core == 1, jnp.where(q == last, 0, q + 1), jnp.where(q == 0, last, q - 1)),
    )
    ninth_from = device(
        jnp.where(core == 0, jnp.where(q == 0, gx(p + 1), p), jnp.where(q == last, gx(p - 1), p)),
        jnp.where(core == 0, jnp.where(q == 0, last, q - 1), jnp.where(q == last, 0, q + 1)),
    )

    shared_to = device(
        jnp.where(core == 0, jnp.where(q == last - 1, gx(p - 1), p), jnp.where(q == 1, gx(p + 1), p)),
        jnp.where(core == 0, jnp.where(q == last - 1, 0, q + 2), jnp.where(q == 1, last, q - 2)),
    )
    shared_from = device(
        jnp.where(core == 0, jnp.where(q == 0, gx(p + 1), p), jnp.where(q == last, gx(p - 1), p)),
        jnp.where(core == 0, jnp.where(q == 0, last - 1, q - 2), jnp.where(q == last, 1, q + 2)),
    )

    barrier = pltpu.get_barrier_semaphore()
    for source in (up, down, sibling, ninth_from, shared_from):
        pl.semaphore_signal(barrier, inc=1, device_id=source, device_id_type=MESH)
    pl.semaphore_wait(barrier, 5)

    def piece(j):
        return pl.ds(pl.multiple_of(j * part, part), part)

    def half_of(h):
        return pl.ds(pl.multiple_of(h * half, half), half)

    def landing(kind, n):
        return buf.at[kind * HOPS + lax.div(n, PIECES), piece(lax.rem(n, PIECES))]

    def ring_copy(kind, n, src):
        return pltpu.make_async_remote_copy(
            src_ref=src,
            dst_ref=landing(kind, n),
            send_sem=ring_send.at[kind, lax.rem(n, SEMS)],
            recv_sem=ring_recv.at[kind, n],
            device_id=up if kind == TXT else down,
            device_id_type=MESH,
        )

    def x_copy(slot, j, src, target):
        return pltpu.make_async_remote_copy(
            src_ref=src,
            dst_ref=buf.at[X_AT + slot, piece(j)],
            send_sem=x_send.at[slot, j],
            recv_sem=x_recv.at[slot, j],
            device_id=target,
            device_id_type=MESH,
        )

    def to_share(k, src):
        return pltpu.make_async_remote_copy(
            src_ref=src,
            dst_ref=shared.at[k],
            send_sem=shared_send.at[k],
            recv_sem=shared_recv.at[k],
            device_id=sibling,
            device_id_type=MESH,
        )

    def pass_shared(k):
        to_share(k, shared.at[k]).wait_recv()
        x_copy(3, k + OWN_NINTH, shared.at[k], shared_to).start()

    inputs = (txt_ref, img_ref)
    short = core

    def set_out(n):
        n = jnp.int32(n)
        for kind in (TXT, IMG):
            ring_copy(kind, n, inputs[kind].at[piece(n)]).start()

    def unit(raw):
        wide = raw.astype(F32)
        return wide * lax.rsqrt(jnp.sum(wide * wide, axis=-1, keepdims=True) + 1e-06)

    def normalize_own(kind):
        def some_rows(i, _):
            at = pl.ds(pl.multiple_of(i * FIN_ROWS, FIN_ROWS), FIN_ROWS)
            own_n[kind, at] = unit(buf[OWN_AT + kind, at]).astype(BF16)
            return 0

        lax.fori_loop(0, rows_here // FIN_ROWS, some_rows, 0)

    set_out(0)
    own_loads = [
        pltpu.make_async_copy(inputs[kind], buf.at[OWN_AT + kind], local_sem.at[kind])
        for kind in (TXT, IMG)
    ]
    for load in own_loads:
        load.start()
    scale, offset = scale_ref[0], offset_ref[0]
    acc[...] = jnp.zeros_like(acc)
    loss_acc[...] = jnp.zeros_like(loss_acc)
    set_out(1)
    for load in own_loads:
        load.wait()
    normalize_own(TXT)
    set_out(2)
    normalize_own(IMG)
    set_out(3)

    def weigh(h, own_pair, with_loss):
        def some_rows(i, _):
            at = pl.ds(pl.multiple_of(i * SUB, SUB), SUB)
            drive = scale * scores[at] + offset
            weight = scale
            if own_pair:
                row = lax.broadcasted_iota(jnp.int32, drive.shape, 0) + i * SUB
                match = row == lax.broadcasted_iota(jnp.int32, drive.shape, 1) + h * half
                drive = jnp.where(match, -drive, drive)
                weight = jnp.where(match, -scale, scale)
            power = jnp.exp(drive)
            coef[at] = (weight * (power * (1.0 / (1.0 + power)))).astype(BF16)
            if with_loss:
                loss = jnp.log1p(power)
                fold = half // 2
                loss_acc[at] += loss[:, :fold] + loss[:, fold:]
            return 0

        lax.fori_loop(0, rows_here // SUB, some_rows, 0, unroll=2)

    def visit(slot, h, kind, own_pair):
        def some_rows(i, _):
            at = pl.ds(pl.multiple_of(h * half + i * FIN_ROWS, FIN_ROWS), FIN_ROWS)
            to = pl.ds(pl.multiple_of(i * FIN_ROWS, FIN_ROWS), FIN_ROWS)
            block[to] = unit(buf[slot, at]).astype(BF16)
            return 0

        lax.fori_loop(0, half // FIN_ROWS, some_rows, 0, unroll=4)
        for r in range(HALVES):
            at = pl.ds(r * half, half)
            scores[at] = lax.dot_general(
                own_n[1 - kind, at], block[...], (((1,), (1,)), ((), ())), preferred_element_type=F32
            )
        for one in (TXT, IMG):

            @pl.when(jnp.logical_and(own_pair, kind == one))
            def _():
                weigh(h, True, one == TXT)

            @pl.when(jnp.logical_and(jnp.logical_not(own_pair), kind == one))
            def _():
                weigh(h, False, one == TXT)

        for r in range(HALVES):
            at = pl.ds(r * half, half)
            acc[kind, at] += jnp.dot(coef[at], block[...], preferred_element_type=F32)

    def finish(kind):
        def some_rows(i, _):
            at = pl.ds(pl.multiple_of(i * FIN_ROWS, FIN_ROWS), FIN_ROWS)
            direction = acc[kind, at]
            raw = buf[OWN_AT + 1 - kind, at].astype(F32)
            inverse = lax.rsqrt(jnp.sum(raw * raw, axis=-1, keepdims=True) + 1e-06)
            along = jnp.sum(raw * direction, axis=-1, keepdims=True) * (inverse * inverse * inverse)
            grads_ref[kind, at] = (inverse * direction - along * raw).astype(BF16)
            return 0

        lax.fori_loop(0, rows_here // FIN_ROWS, some_rows, 0, unroll=4)

    def within(i, low, count):
        return jnp.logical_and(i >= low, i < low + count)

    ending = sends - 3

    def turn(i, _):
        t = jnp.where(i > ending, i - 1, i)

        @pl.when(jnp.logical_and(t < sends, i != ending + 1))
        def _():
            onward = t + PIECES
            j = lax.rem(t, PIECES)
            for kind in (TXT, IMG):
                ring_copy(kind, t, landing(kind, t)).wait_recv()

                @pl.when(onward < sends)
                def _():
                    ring_copy(kind, onward, landing(kind, t)).start()

                @pl.when(jnp.logical_and(within(onward, sends, OWN_NINTH), short != kind))
                def _():
                    x_copy(3, j, landing(kind, t), ninth_to).start()

                @pl.when(jnp.logical_and(onward >= sends + OWN_NINTH, short != kind))
                def _():
                    to_share(j - OWN_NINTH, landing(kind, t)).start()

                @pl.when(jnp.logical_and(onward >= sends, short == kind))
                def _():
                    x_copy(1, j, landing(kind, t), sibling).start()

                @pl.when(jnp.logical_and(t < PIECES, short != kind))
                def _():
                    x_copy(2, j, landing(kind, t), sibling).start()

                @pl.when(jnp.logical_and(t < PIECES, short == kind))
                def _():
                    x_copy(0, j, inputs[kind].at[piece(j)], sibling).start()

                @pl.when(t >= PIECES)
                def _():
                    ring_copy(kind, t - PIECES, landing(kind, t)).wait_send()

        since = i - ending

        for k in range(PIECES - OWN_NINTH):

            @pl.when(since == k + 3)
            def _():
                pass_shared(k)

        @pl.when(since == 7)
        def _():
            finish(1 - core)

        is_end = since >= 0
        is_own = i < 4
        is_x_early = within(i, 4, 4)
        step = lax.rem(jnp.maximum(since, 0), 3)
        is_x3 = since >= 6
        is_x1 = jnp.logical_and(within(since, 0, 6), step == 2)
        is_x = jnp.logical_or(is_x_early, jnp.logical_or(is_x1, is_x3))
        x_slot = jnp.where(is_x3, 3, jnp.where(is_x1, 1, jnp.where(i < 6, 0, 2)))
        kind = jnp.where(
            is_x, jnp.where(x_slot < 2, 1 - core, core), jnp.where(is_end, step, lax.rem(i, 2))
        )
        slot = jnp.where(
            is_x, X_AT + x_slot, jnp.where(is_end, kind * HOPS + HOPS - 1, OWN_AT + kind)
        )
        h = jnp.where(
            is_end,
            jnp.where(is_x3, since - 6, jnp.where(since >= 3, 1, 0)),
            jnp.where(is_own, lax.div(i, 2), lax.rem(i, 2)),
        )

        @pl.when(is_x)
        def _():
            for k in range(PIECES // HALVES):
                j = h * (PIECES // HALVES) + k
                x_copy(x_slot, j, buf.at[X_AT, piece(j)], sibling).wait_recv()

        @pl.when(jnp.logical_or(is_end, i < 8))
        def _():
            visit(slot, h, kind, is_own)

        return 0

    lax.fori_loop(0, ending + 8, turn, 0)
    finish(core)
    loss_ref[...] = jnp.sum(loss_acc[...].T, axis=0, keepdims=True) / (4.0 * rows_here)

    for k in range(PIECES - OWN_NINTH):
        to_share(k, shared.at[k]).wait_send()

    def drain(j, _):
        for slot in range(4):
            x_copy(slot, j, buf.at[X_AT, piece(j)], sibling).wait_send()
        for kind in (TXT, IMG):
            n = sends - PIECES + j
            ring_copy(kind, n, landing(kind, n)).wait_send()
        return 0

    lax.fori_loop(0, PIECES, drain, 0)


def hand_out(grads_ref, loss_in, img_out, txt_out, loss_out, sems):
    copies = [
        pltpu.make_async_copy(grads_ref.at[one], out, sems.at[one])
        for one, out in ((TXT, img_out), (IMG, txt_out))
    ]
    for copy in copies:
        copy.start()
    loss_out[...] = loss_in[...]
    for copy in copies:
        copy.wait()


def solution(mesh):
    n_gx, n_gy = mesh.shape["gx"], mesh.shape["gy"]

    def body(img, txt, scale, offset):
        rows, width = img.shape
        half = rows // HALVES
        sends = HOPS * PIECES

        def run(*refs):
            kernel(n_gx, n_gy, *refs)

        any_space = pl.BlockSpec(memory_space=pl.ANY)
        smem = pl.BlockSpec(memory_space=pltpu.SMEM)
        vmem = pl.BlockSpec(memory_space=pltpu.VMEM)
        grads, loss = pl.pallas_call(
            run,
            out_shape=(pltpu.VMEM((2, rows, width), BF16), pltpu.VMEM((1, rows), F32)),
            in_specs=[any_space, any_space, smem, smem],
            out_specs=(vmem, vmem),
            scratch_shapes=[
                pltpu.VMEM((N_SLOTS, rows, width), BF16),
                pltpu.VMEM((2, rows, width), BF16),
                pltpu.VMEM((2, rows, width), F32),
                pltpu.VMEM((rows, half // 2), F32),
                pltpu.VMEM((half, width), BF16),
                pltpu.VMEM((rows, half), F32),
                pltpu.VMEM((rows, half), BF16),
                pltpu.VMEM((PIECES - OWN_NINTH, rows // PIECES, width), BF16),
                pltpu.SemaphoreType.DMA((PIECES - OWN_NINTH,)),
                pltpu.SemaphoreType.DMA((PIECES - OWN_NINTH,)),
                pltpu.SemaphoreType.DMA((2, SEMS)),
                pltpu.SemaphoreType.DMA((2, sends)),
                pltpu.SemaphoreType.DMA((4, PIECES)),
                pltpu.SemaphoreType.DMA((4, PIECES)),
                pltpu.SemaphoreType.DMA((2,)),
            ],
            compiler_params=pltpu.CompilerParams(
                collective_id=0, has_side_effects=True, vmem_limit_bytes=52 * 1024 * 1024
            ),
            cost_estimate=pl.CostEstimate(
                flops=14 * 2 * rows * rows * width, bytes_accessed=8 * rows * width, transcendentals=0
            ),
        )(img, txt, scale, offset)
        img_grad, txt_grad, loss = pl.pallas_call(
            hand_out,
            out_shape=(
                jax.ShapeDtypeStruct((rows, width), BF16),
                jax.ShapeDtypeStruct((rows, width), BF16),
                jax.ShapeDtypeStruct((1, rows), F32),
            ),
            in_specs=[vmem, vmem],
            out_specs=(any_space, any_space, vmem),
            scratch_shapes=[pltpu.SemaphoreType.DMA((2,))],
            compiler_params=pltpu.CompilerParams(vmem_limit_bytes=4 * 1024 * 1024),
        )(grads, loss)
        return loss.reshape(rows), img_grad, txt_grad

    return jax.shard_map(
        body,
        mesh=mesh,
        in_specs=(P(("gx", "gy"), None), P(("gx", "gy"), None), P(), P()),
        out_specs=(P(("gx", "gy")), P(("gx", "gy"), None), P(("gx", "gy"), None)),
        check_vma=False,
    )
```

```python
import jax
import jax.numpy as jnp
from jax import lax
from jax.experimental import pallas as pl
from jax.experimental.pallas import tpu as pltpu
from jax.sharding import PartitionSpec as P

MESH = pl.DeviceIdType.MESH
F32 = jnp.float32
BF16 = jnp.bfloat16

TXT, IMG = 0, 1
HOPS = 8
PIECES = 4
HALVES = 2
SEMS = 16
SUB = 64
FIN_ROWS = 32

X_AT = 2 * HOPS
OWN_AT = X_AT + 4
N_SLOTS = OWN_AT + 2


def kernel(
    n_gx,
    n_gy,
    img_ref,
    txt_ref,
    scale_ref,
    offset_ref,
    grads_ref,
    loss_ref,
    buf,
    own_n,
    acc,
    loss_acc,
    block,
    scores,
    coef,
    ring_send,
    ring_recv,
    x_send,
    x_recv,
    local_sem,
):
    rows_here, width = img_ref.shape
    part, half = rows_here // PIECES, rows_here // HALVES
    sends = HOPS * PIECES
    p, q = lax.axis_index("gx"), lax.axis_index("gy")
    core = lax.rem(q, 2)
    last = n_gy - 1

    def gx(value):
        return lax.rem(value + n_gx, n_gx)

    def device(gx_index, gy_index):
        return (gx_index, gy_index)

    wraps_up = q >= n_gy - 2
    wraps_down = q < 2
    up = device(jnp.where(wraps_up, gx(p + 1), p), jnp.where(wraps_up, core, q + 2))
    down = device(jnp.where(wraps_down, gx(p - 1), p), jnp.where(wraps_down, n_gy - 2 + core, q - 2))
    sibling = device(p, q + 1 - 2 * core)
    ninth_to = device(
        jnp.where(core == 1, jnp.where(q == last, gx(p - 1), p), jnp.where(q == 0, gx(p + 1), p)),
        jnp.where(core == 1, jnp.where(q == last, 0, q + 1), jnp.where(q == 0, last, q - 1)),
    )
    ninth_from = device(
        jnp.where(core == 0, jnp.where(q == 0, gx(p + 1), p), jnp.where(q == last, gx(p - 1), p)),
        jnp.where(core == 0, jnp.where(q == 0, last, q - 1), jnp.where(q == last, 0, q + 1)),
    )

    barrier = pltpu.get_barrier_semaphore()
    for source in (up, down, sibling, ninth_from):
        pl.semaphore_signal(barrier, inc=1, device_id=source, device_id_type=MESH)
    pl.semaphore_wait(barrier, 4)

    def piece(j):
        return pl.ds(pl.multiple_of(j * part, part), part)

    def half_of(h):
        return pl.ds(pl.multiple_of(h * half, half), half)

    def landing(kind, n):
        return buf.at[kind * HOPS + lax.div(n, PIECES), piece(lax.rem(n, PIECES))]

    def ring_copy(kind, n, src):
        return pltpu.make_async_remote_copy(
            src_ref=src,
            dst_ref=landing(kind, n),
            send_sem=ring_send.at[kind, lax.rem(n, SEMS)],
            recv_sem=ring_recv.at[kind, n],
            device_id=up if kind == TXT else down,
            device_id_type=MESH,
        )

    def x_copy(slot, j, src, target):
        return pltpu.make_async_remote_copy(
            src_ref=src,
            dst_ref=buf.at[X_AT + slot, piece(j)],
            send_sem=x_send.at[slot, j],
            recv_sem=x_recv.at[slot, j],
            device_id=target,
            device_id_type=MESH,
        )

    inputs = (txt_ref, img_ref)
    short = core

    def set_out(n):
        n = jnp.int32(n)
        for kind in (TXT, IMG):
            ring_copy(kind, n, inputs[kind].at[piece(n)]).start()

    def unit(raw):
        wide = raw.astype(F32)
        return wide * lax.rsqrt(jnp.sum(wide * wide, axis=-1, keepdims=True) + 1e-06)

    def normalize_own(kind):
        def some_rows(i, _):
            at = pl.ds(pl.multiple_of(i * FIN_ROWS, FIN_ROWS), FIN_ROWS)
            own_n[kind, at] = unit(buf[OWN_AT + kind, at]).astype(BF16)
            return 0

        lax.fori_loop(0, rows_here // FIN_ROWS, some_rows, 0)

    set_out(0)
    own_loads = [
        pltpu.make_async_copy(inputs[kind], buf.at[OWN_AT + kind], local_sem.at[kind])
        for kind in (TXT, IMG)
    ]
    for load in own_loads:
        load.start()
    scale, offset = scale_ref[0], offset_ref[0]
    acc[...] = jnp.zeros_like(acc)
    loss_acc[...] = jnp.zeros_like(loss_acc)
    set_out(1)
    for load in own_loads:
        load.wait()
    normalize_own(TXT)
    set_out(2)
    normalize_own(IMG)
    set_out(3)

    def weigh(h, size, own_pair, with_loss):
        def some_rows(i, _):
            at = pl.ds(pl.multiple_of(i * SUB, SUB), SUB)
            drive = scale * scores[at, :size] + offset
            weight = scale
            if own_pair:
                row = lax.broadcasted_iota(jnp.int32, drive.shape, 0) + i * SUB
                match = row == lax.broadcasted_iota(jnp.int32, drive.shape, 1) + h * half
                drive = jnp.where(match, -drive, drive)
                weight = jnp.where(match, -scale, scale)
            power = jnp.exp(drive)
            coef[at, :size] = (weight * (power * (1.0 / (1.0 + power)))).astype(BF16)
            if with_loss:
                loss = jnp.log1p(power)
                loss_acc[at] += loss if size == part else loss[:, :part] + loss[:, part:]
            return 0

        lax.fori_loop(0, rows_here // SUB, some_rows, 0, unroll=2)

    def visit(slot, h, size, kind, own_pair):
        def some_rows(i, _):
            at = pl.ds(pl.multiple_of(h * size + i * FIN_ROWS, FIN_ROWS), FIN_ROWS)
            to = pl.ds(pl.multiple_of(i * FIN_ROWS, FIN_ROWS), FIN_ROWS)
            block[to] = unit(buf[slot, at]).astype(BF16)
            return 0

        lax.fori_loop(0, size // FIN_ROWS, some_rows, 0, unroll=min(4, size // FIN_ROWS))
        for r in range(HALVES):
            at = pl.ds(r * half, half)
            scores[at, :size] = lax.dot_general(
                own_n[1 - kind, at],
                block[:size],
                (((1,), (1,)), ((), ())),
                preferred_element_type=F32,
            )
        for one in (TXT, IMG):
            if own_pair is not False:

                @pl.when(jnp.logical_and(own_pair, kind == one))
                def _():
                    weigh(h, size, True, one == TXT)

            @pl.when(jnp.logical_and(jnp.logical_not(own_pair), kind == one))
            def _():
                weigh(h, size, False, one == TXT)

        for r in range(HALVES):
            at = pl.ds(r * half, half)
            acc[kind, at] += jnp.dot(coef[at, :size], block[:size], preferred_element_type=F32)

    def finish(kind):
        def some_rows(i, _):
            at = pl.ds(pl.multiple_of(i * FIN_ROWS, FIN_ROWS), FIN_ROWS)
            direction = acc[kind, at]
            raw = buf[OWN_AT + 1 - kind, at].astype(F32)
            inverse = lax.rsqrt(jnp.sum(raw * raw, axis=-1, keepdims=True) + 1e-06)
            along = jnp.sum(raw * direction, axis=-1, keepdims=True) * (inverse * inverse * inverse)
            grads_ref[kind, at] = (inverse * direction - along * raw).astype(BF16)
            return 0

        lax.fori_loop(0, rows_here // FIN_ROWS, some_rows, 0, unroll=4)

    def within(i, low, count):
        return jnp.logical_and(i >= low, i < low + count)

    def drain(j, _):
        for slot in range(3):
            x_copy(slot, j, buf.at[X_AT, piece(j)], sibling).wait_send()
        for kind in (TXT, IMG):
            n = sends - PIECES + j
            ring_copy(kind, n, landing(kind, n)).wait_send()
        return 0

    ending = sends - 3

    def turn(i, _):
        t = jnp.where(i > ending, i - 1, i)

        @pl.when(jnp.logical_and(t < sends, i != ending + 1))
        def _():
            onward = t + PIECES
            j = lax.rem(t, PIECES)
            for kind in (TXT, IMG):
                ring_copy(kind, t, landing(kind, t)).wait_recv()

                @pl.when(onward < sends)
                def _():
                    ring_copy(kind, onward, landing(kind, t)).start()

                @pl.when(jnp.logical_and(onward >= sends, short != kind))
                def _():
                    x_copy(3, j, landing(kind, t), ninth_to).start()

                @pl.when(jnp.logical_and(onward >= sends, short == kind))
                def _():
                    x_copy(1, j, landing(kind, t), sibling).start()

                @pl.when(jnp.logical_and(t < PIECES, short != kind))
                def _():
                    x_copy(2, j, landing(kind, t), sibling).start()

                @pl.when(jnp.logical_and(t < PIECES, short == kind))
                def _():
                    x_copy(0, j, inputs[kind].at[piece(j)], sibling).start()

                @pl.when(t >= PIECES)
                def _():
                    ring_copy(kind, t - PIECES, landing(kind, t)).wait_send()

        since = i - ending

        @pl.when(since == 7)
        def _():
            finish(1 - core)
            lax.fori_loop(0, PIECES, drain, 0)

        is_end = since >= 0
        is_own = i < 4
        is_x_early = within(i, 4, 4)
        step = lax.rem(jnp.maximum(since, 0), 3)
        is_x3 = since >= 6
        is_x1 = jnp.logical_and(within(since, 0, 6), step == 2)
        is_x = jnp.logical_or(is_x_early, jnp.logical_or(is_x1, is_x3))
        x_slot = jnp.where(is_x3, 3, jnp.where(is_x1, 1, jnp.where(i < 6, 0, 2)))
        kind = jnp.where(
            is_x, jnp.where(x_slot < 2, 1 - core, core), jnp.where(is_end, step, lax.rem(i, 2))
        )
        slot = jnp.where(
            is_x, X_AT + x_slot, jnp.where(is_end, kind * HOPS + HOPS - 1, OWN_AT + kind)
        )
        h = jnp.where(
            is_end,
            jnp.where(is_x3, since - 6, jnp.where(since >= 3, 1, 0)),
            jnp.where(is_own, lax.div(i, 2), lax.rem(i, 2)),
        )

        @pl.when(jnp.logical_and(is_x, since <= 6))
        def _():
            for k in range(PIECES // HALVES):
                j = h * (PIECES // HALVES) + k
                x_copy(x_slot, j, buf.at[X_AT, piece(j)], sibling).wait_recv()

        @pl.when(jnp.logical_or(within(since, 0, 7), i < 8))
        def _():
            visit(slot, h, half, kind, is_own)

        @pl.when(since >= 7)
        def _():
            j = since - 7 + PIECES // HALVES
            x_copy(3, j, buf.at[X_AT, piece(j)], sibling).wait_recv()
            visit(X_AT + 3, j, part, core, False)

        return 0

    lax.fori_loop(0, ending + 7 + PIECES // HALVES, turn, 0)
    finish(core)
    loss_ref[...] = jnp.sum(loss_acc[...].T, axis=0, keepdims=True) / (4.0 * rows_here)

    for j in range(PIECES):
        x_copy(3, j, buf.at[X_AT, piece(j)], sibling).wait_send()


def hand_out(grads_ref, loss_in, img_out, txt_out, loss_out, sems):
    part = img_out.shape[0] // PIECES
    copies = [
        pltpu.make_async_copy(
            grads_ref.at[one, pl.ds(j * part, part)], out.at[pl.ds(j * part, part)], sems.at[one, j]
        )
        for j in range(PIECES)
        for one, out in ((TXT, img_out), (IMG, txt_out))
    ]
    for copy in copies:
        copy.start()
    loss_out[...] = loss_in[...]
    for copy in copies:
        copy.wait()


def solution(mesh):
    n_gx, n_gy = mesh.shape["gx"], mesh.shape["gy"]

    def body(img, txt, scale, offset):
        rows, width = img.shape
        half = rows // HALVES
        sends = HOPS * PIECES

        def run(*refs):
            kernel(n_gx, n_gy, *refs)

        any_space = pl.BlockSpec(memory_space=pl.ANY)
        smem = pl.BlockSpec(memory_space=pltpu.SMEM)
        vmem = pl.BlockSpec(memory_space=pltpu.VMEM)
        grads, loss = pl.pallas_call(
            run,
            out_shape=(pltpu.VMEM((2, rows, width), BF16), pltpu.VMEM((1, rows), F32)),
            in_specs=[any_space, any_space, smem, smem],
            out_specs=(vmem, vmem),
            scratch_shapes=[
                pltpu.VMEM((N_SLOTS, rows, width), BF16),
                pltpu.VMEM((2, rows, width), BF16),
                pltpu.VMEM((2, rows, width), F32),
                pltpu.VMEM((rows, half // 2), F32),
                pltpu.VMEM((half, width), BF16),
                pltpu.VMEM((rows, half), F32),
                pltpu.VMEM((rows, half), BF16),
                pltpu.SemaphoreType.DMA((2, SEMS)),
                pltpu.SemaphoreType.DMA((2, sends)),
                pltpu.SemaphoreType.DMA((4, PIECES)),
                pltpu.SemaphoreType.DMA((4, PIECES)),
                pltpu.SemaphoreType.DMA((2,)),
            ],
            compiler_params=pltpu.CompilerParams(
                collective_id=0, has_side_effects=True, vmem_limit_bytes=52 * 1024 * 1024
            ),
            cost_estimate=pl.CostEstimate(
                flops=14 * 2 * rows * rows * width, bytes_accessed=8 * rows * width, transcendentals=0
            ),
        )(img, txt, scale, offset)
        img_grad, txt_grad, loss = pl.pallas_call(
            hand_out,
            out_shape=(
                jax.ShapeDtypeStruct((rows, width), BF16),
                jax.ShapeDtypeStruct((rows, width), BF16),
                jax.ShapeDtypeStruct((1, rows), F32),
            ),
            in_specs=[vmem, vmem],
            out_specs=(any_space, any_space, vmem),
            scratch_shapes=[pltpu.SemaphoreType.DMA((2, PIECES))],
            compiler_params=pltpu.CompilerParams(vmem_limit_bytes=4 * 1024 * 1024),
        )(grads, loss)
        return loss.reshape(rows), img_grad, txt_grad

    return jax.shard_map(
        body,
        mesh=mesh,
        in_specs=(P(("gx", "gy"), None), P(("gx", "gy"), None), P(), P()),
        out_specs=(P(("gx", "gy")), P(("gx", "gy"), None), P(("gx", "gy"), None)),
        check_vma=False,
    )
```

```python
import jax
import jax.numpy as jnp
from jax import lax
from jax.experimental import pallas as pl
from jax.experimental.pallas import tpu as pltpu
from jax.sharding import PartitionSpec as P

MESH = pl.DeviceIdType.MESH
F32 = jnp.float32
BF16 = jnp.bfloat16

TXT, IMG = 0, 1
HOPS = 8
PIECES = 4
HALVES = 2
SEMS = 16
SUB = 64
FIN_ROWS = 32

X_AT = 2 * HOPS
OWN_AT = X_AT + 4
N_SLOTS = OWN_AT + 2


def kernel(
    n_gx,
    n_gy,
    img_ref,
    txt_ref,
    scale_ref,
    offset_ref,
    grads_ref,
    loss_ref,
    buf,
    own_n,
    acc,
    loss_acc,
    block,
    scores,
    coef,
    ring_send,
    ring_recv,
    x_send,
    x_recv,
    local_sem,
):
    rows_here, width = img_ref.shape
    part, half = rows_here // PIECES, rows_here // HALVES
    sends = HOPS * PIECES
    p, q = lax.axis_index("gx"), lax.axis_index("gy")
    core = lax.rem(q, 2)
    last = n_gy - 1

    def gx(value):
        return lax.rem(value + n_gx, n_gx)

    def device(gx_index, gy_index):
        return (gx_index, gy_index)

    wraps_up = q >= n_gy - 2
    wraps_down = q < 2
    up = device(jnp.where(wraps_up, gx(p + 1), p), jnp.where(wraps_up, core, q + 2))
    down = device(jnp.where(wraps_down, gx(p - 1), p), jnp.where(wraps_down, n_gy - 2 + core, q - 2))
    sibling = device(p, q + 1 - 2 * core)
    ninth_to = device(
        jnp.where(core == 1, jnp.where(q == last, gx(p - 1), p), jnp.where(q == 0, gx(p + 1), p)),
        jnp.where(core == 1, jnp.where(q == last, 0, q + 1), jnp.where(q == 0, last, q - 1)),
    )
    ninth_from = device(
        jnp.where(core == 0, jnp.where(q == 0, gx(p + 1), p), jnp.where(q == last, gx(p - 1), p)),
        jnp.where(core == 0, jnp.where(q == 0, last, q - 1), jnp.where(q == last, 0, q + 1)),
    )

    barrier = pltpu.get_barrier_semaphore()
    for source in (up, down, sibling, ninth_from):
        pl.semaphore_signal(barrier, inc=1, device_id=source, device_id_type=MESH)
    pl.semaphore_wait(barrier, 4)

    def piece(j):
        return pl.ds(pl.multiple_of(j * part, part), part)

    def half_of(h):
        return pl.ds(pl.multiple_of(h * half, half), half)

    def landing(kind, n):
        return buf.at[kind * HOPS + lax.div(n, PIECES), piece(lax.rem(n, PIECES))]

    def ring_copy(kind, n, src):
        return pltpu.make_async_remote_copy(
            src_ref=src,
            dst_ref=landing(kind, n),
            send_sem=ring_send.at[kind, lax.rem(n, SEMS)],
            recv_sem=ring_recv.at[kind, n],
            device_id=up if kind == TXT else down,
            device_id_type=MESH,
        )

    def x_copy(slot, j, src, target):
        return pltpu.make_async_remote_copy(
            src_ref=src,
            dst_ref=buf.at[X_AT + slot, piece(j)],
            send_sem=x_send.at[slot, j],
            recv_sem=x_recv.at[slot, j],
            device_id=target,
            device_id_type=MESH,
        )

    inputs = (txt_ref, img_ref)
    short = core

    def set_out(n):
        n = jnp.int32(n)
        for kind in (TXT, IMG):
            ring_copy(kind, n, inputs[kind].at[piece(n)]).start()

    def unit(raw):
        wide = raw.astype(F32)
        return wide * lax.rsqrt(jnp.sum(wide * wide, axis=-1, keepdims=True) + 1e-06)

    def normalize_own(kind):
        def some_rows(i, _):
            at = pl.ds(pl.multiple_of(i * FIN_ROWS, FIN_ROWS), FIN_ROWS)
            own_n[kind, at] = unit(buf[OWN_AT + kind, at]).astype(BF16)
            return 0

        lax.fori_loop(0, rows_here // FIN_ROWS, some_rows, 0)

    for n in range(PIECES):
        set_out(n)
    own_loads = [
        pltpu.make_async_copy(inputs[kind], buf.at[OWN_AT + kind], local_sem.at[kind])
        for kind in (TXT, IMG)
    ]
    for load in own_loads:
        load.start()
    scale, offset = scale_ref[0], offset_ref[0]
    acc[...] = jnp.zeros_like(acc)
    loss_acc[...] = jnp.zeros_like(loss_acc)
    for load in own_loads:
        load.wait()
    normalize_own(TXT)
    normalize_own(IMG)

    def weigh(h, size, own_pair, with_loss):
        def some_rows(i, _):
            at = pl.ds(pl.multiple_of(i * SUB, SUB), SUB)
            drive = scale * scores[at, :size] + offset
            weight = scale
            if own_pair:
                row = lax.broadcasted_iota(jnp.int32, drive.shape, 0) + i * SUB
                match = row == lax.broadcasted_iota(jnp.int32, drive.shape, 1) + h * half
                drive = jnp.where(match, -drive, drive)
                weight = jnp.where(match, -scale, scale)
            power = jnp.exp(drive)
            coef[at, :size] = (weight * (power * (1.0 / (1.0 + power)))).astype(BF16)
            if with_loss:
                loss = jnp.log1p(power)
                loss_acc[at] += loss if size == part else loss[:, :part] + loss[:, part:]
            return 0

        lax.fori_loop(0, rows_here // SUB, some_rows, 0, unroll=2)

    def visit(slot, h, size, kind, own_pair):
        def some_rows(i, _):
            at = pl.ds(pl.multiple_of(h * size + i * FIN_ROWS, FIN_ROWS), FIN_ROWS)
            to = pl.ds(pl.multiple_of(i * FIN_ROWS, FIN_ROWS), FIN_ROWS)
            block[to] = unit(buf[slot, at]).astype(BF16)
            return 0

        lax.fori_loop(0, size // FIN_ROWS, some_rows, 0, unroll=min(4, size // FIN_ROWS))
        for r in range(HALVES):
            at = pl.ds(r * half, half)
            scores[at, :size] = lax.dot_general(
                own_n[1 - kind, at],
                block[:size],
                (((1,), (1,)), ((), ())),
                preferred_element_type=F32,
            )
        for one in (TXT, IMG):
            if own_pair is not False:

                @pl.when(jnp.logical_and(own_pair, kind == one))
                def _():
                    weigh(h, size, True, one == TXT)

            @pl.when(jnp.logical_and(jnp.logical_not(own_pair), kind == one))
            def _():
                weigh(h, size, False, one == TXT)

        for r in range(HALVES):
            at = pl.ds(r * half, half)
            acc[kind, at] += jnp.dot(coef[at, :size], block[:size], preferred_element_type=F32)

    def finish(kind):
        def some_rows(i, _):
            at = pl.ds(pl.multiple_of(i * FIN_ROWS, FIN_ROWS), FIN_ROWS)
            direction = acc[kind, at]
            raw = buf[OWN_AT + 1 - kind, at].astype(F32)
            inverse = lax.rsqrt(jnp.sum(raw * raw, axis=-1, keepdims=True) + 1e-06)
            along = jnp.sum(raw * direction, axis=-1, keepdims=True) * (inverse * inverse * inverse)
            grads_ref[kind, at] = (inverse * direction - along * raw).astype(BF16)
            return 0

        lax.fori_loop(0, rows_here // FIN_ROWS, some_rows, 0, unroll=4)

    def within(i, low, count):
        return jnp.logical_and(i >= low, i < low + count)

    def drain(j, _):
        for slot in range(3):
            x_copy(slot, j, buf.at[X_AT, piece(j)], sibling).wait_send()
        for kind in (TXT, IMG):
            n = sends - PIECES + j
            ring_copy(kind, n, landing(kind, n)).wait_send()
        return 0

    ending = sends - 3

    def turn(i, _):
        t = jnp.where(i > ending, i - 1, i)

        @pl.when(jnp.logical_and(t < sends, i != ending + 1))
        def _():
            onward = t + PIECES
            j = lax.rem(t, PIECES)
            for kind in (TXT, IMG):
                ring_copy(kind, t, landing(kind, t)).wait_recv()

                @pl.when(onward < sends)
                def _():
                    ring_copy(kind, onward, landing(kind, t)).start()

                @pl.when(jnp.logical_and(onward >= sends, short != kind))
                def _():
                    x_copy(3, j, landing(kind, t), ninth_to).start()

                @pl.when(jnp.logical_and(onward >= sends, short == kind))
                def _():
                    x_copy(1, j, landing(kind, t), sibling).start()

                @pl.when(jnp.logical_and(t < PIECES, short != kind))
                def _():
                    x_copy(2, j, landing(kind, t), sibling).start()

                @pl.when(jnp.logical_and(t < PIECES, short == kind))
                def _():
                    x_copy(0, j, inputs[kind].at[piece(j)], sibling).start()

                @pl.when(t >= PIECES)
                def _():
                    ring_copy(kind, t - PIECES, landing(kind, t)).wait_send()

        since = i - ending

        @pl.when(since == 7)
        def _():
            finish(1 - core)
            lax.fori_loop(0, PIECES, drain, 0)

        is_end = since >= 0
        is_own = i < 4
        is_x_early = within(i, 4, 4)
        step = lax.rem(jnp.maximum(since, 0), 3)
        is_x3 = since >= 6
        is_x1 = jnp.logical_and(within(since, 0, 6), step == 2)
        is_x = jnp.logical_or(is_x_early, jnp.logical_or(is_x1, is_x3))
        x_slot = jnp.where(is_x3, 3, jnp.where(is_x1, 1, jnp.where(i < 6, 0, 2)))
        kind = jnp.where(
            is_x, jnp.where(x_slot < 2, 1 - core, core), jnp.where(is_end, step, lax.rem(i, 2))
        )
        slot = jnp.where(
            is_x, X_AT + x_slot, jnp.where(is_end, kind * HOPS + HOPS - 1, OWN_AT + kind)
        )
        h = jnp.where(
            is_end,
            jnp.where(is_x3, since - 6, jnp.where(since >= 3, 1, 0)),
            jnp.where(is_own, lax.div(i, 2), lax.rem(i, 2)),
        )

        @pl.when(jnp.logical_and(is_x, since <= 6))
        def _():
            for k in range(PIECES // HALVES):
                j = h * (PIECES // HALVES) + k
                x_copy(x_slot, j, buf.at[X_AT, piece(j)], sibling).wait_recv()

        @pl.when(jnp.logical_or(within(since, 0, 7), i < 8))
        def _():
            visit(slot, h, half, kind, is_own)

        @pl.when(since >= 7)
        def _():
            j = since - 7 + PIECES // HALVES
            x_copy(3, j, buf.at[X_AT, piece(j)], sibling).wait_recv()
            visit(X_AT + 3, j, part, core, False)

        return 0

    lax.fori_loop(0, ending + 7 + PIECES // HALVES, turn, 0)
    finish(core)
    loss_ref[...] = jnp.sum(loss_acc[...].T, axis=0, keepdims=True) / (4.0 * rows_here)

    for j in range(PIECES):
        x_copy(3, j, buf.at[X_AT, piece(j)], sibling).wait_send()


def hand_out(grads_ref, loss_in, img_out, txt_out, loss_out, sems):
    part = img_out.shape[0] // PIECES
    copies = [
        pltpu.make_async_copy(
            grads_ref.at[one, pl.ds(j * part, part)], out.at[pl.ds(j * part, part)], sems.at[one, j]
        )
        for j in range(PIECES)
        for one, out in ((TXT, img_out), (IMG, txt_out))
    ]
    for copy in copies:
        copy.start()
    loss_out[...] = loss_in[...]
    for copy in copies:
        copy.wait()


def solution(mesh):
    n_gx, n_gy = mesh.shape["gx"], mesh.shape["gy"]

    def body(img, txt, scale, offset):
        rows, width = img.shape
        half = rows // HALVES
        sends = HOPS * PIECES

        def run(*refs):
            kernel(n_gx, n_gy, *refs)

        any_space = pl.BlockSpec(memory_space=pl.ANY)
        smem = pl.BlockSpec(memory_space=pltpu.SMEM)
        vmem = pl.BlockSpec(memory_space=pltpu.VMEM)
        grads, loss = pl.pallas_call(
            run,
            out_shape=(pltpu.VMEM((2, rows, width), BF16), pltpu.VMEM((1, rows), F32)),
            in_specs=[any_space, any_space, smem, smem],
            out_specs=(vmem, vmem),
            scratch_shapes=[
                pltpu.VMEM((N_SLOTS, rows, width), BF16),
                pltpu.VMEM((2, rows, width), BF16),
                pltpu.VMEM((2, rows, width), F32),
                pltpu.VMEM((rows, half // 2), F32),
                pltpu.VMEM((half, width), BF16),
                pltpu.VMEM((rows, half), F32),
                pltpu.VMEM((rows, half), BF16),
                pltpu.SemaphoreType.DMA((2, SEMS)),
                pltpu.SemaphoreType.DMA((2, sends)),
                pltpu.SemaphoreType.DMA((4, PIECES)),
                pltpu.SemaphoreType.DMA((4, PIECES)),
                pltpu.SemaphoreType.DMA((2,)),
            ],
            compiler_params=pltpu.CompilerParams(
                collective_id=0, has_side_effects=True, vmem_limit_bytes=52 * 1024 * 1024
            ),
            cost_estimate=pl.CostEstimate(
                flops=14 * 2 * rows * rows * width, bytes_accessed=8 * rows * width, transcendentals=0
            ),
        )(img, txt, scale, offset)
        img_grad, txt_grad, loss = pl.pallas_call(
            hand_out,
            out_shape=(
                jax.ShapeDtypeStruct((rows, width), BF16),
                jax.ShapeDtypeStruct((rows, width), BF16),
                jax.ShapeDtypeStruct((1, rows), F32),
            ),
            in_specs=[vmem, vmem],
            out_specs=(any_space, any_space, vmem),
            scratch_shapes=[pltpu.SemaphoreType.DMA((2, PIECES))],
            compiler_params=pltpu.CompilerParams(vmem_limit_bytes=4 * 1024 * 1024),
        )(grads, loss)
        return loss.reshape(rows), img_grad, txt_grad

    return jax.shard_map(
        body,
        mesh=mesh,
        in_specs=(P(("gx", "gy"), None), P(("gx", "gy"), None), P(), P()),
        out_specs=(P(("gx", "gy")), P(("gx", "gy"), None), P(("gx", "gy"), None)),
        check_vma=False,
    )
```
